256 devices in a mesh: adapter: 32 (over y, z), tensor: 8 (over x, core).
Axes of the slice: x: 4, y: 4, z: 8, core: 2. Of those that a mesh axis runs over, the one named last changes fastest.
Arguments:
- queries: bfloat16 [1536, 8192], P('adapter', 'tensor'), may hold values from -2000 to 2000
- cache_keys: bfloat16 [1536, 8, 32, 128], P('adapter', 'tensor'), may hold values from -6 to 6
- cache_values: bfloat16 [1536, 8, 32, 128], P('adapter', 'tensor'), may hold values from -6 to 6
- new_keys: bfloat16 [1536, 1024], P('adapter', 'tensor'), may hold values from -7 to 7
- new_values: bfloat16 [1536, 1024], P('adapter', 'tensor'), may hold values from -6 to 6
- cache_lengths: int32 [1536], P('adapter'), may hold values from 1 to 32, as said below
- out_weight: bfloat16 [8192, 4096], P('tensor'), may hold values from -0.0625 to 0.0625
- adapter_down: bfloat16 [8192, 32768], P('tensor', 'adapter'), may hold values from -0.0625 to 0.0625
- adapter_up: bfloat16 [32768, 4096], P('adapter', 'tensor'), may hold values from -0.75 to 0.75
- adapter_ids: int32 [1536, 4], P('adapter'), may hold values from 0 to 511, as said below
- hub_weights: float32 [1536, 4], P('adapter'), may hold values from -1.5 to 1.5
Outputs:
- layer_out: bfloat16 [1536, 4096], P('adapter', 'tensor')
The draws below stay inside these ranges and needn't reach their ends.
Inputs may be any that keep to these rules, and one draw needn't show every extreme that they name: `adapter_ids`: the 4 adapters of a row are distinct; adapter a is held by index a // 16 of the adapter axis. Among the 192 row-adapter pairs of one device's rows at most 24 name adapters held by one index, and in every draw one index takes exactly 24 pairs from every device. `cache_lengths`: among each device's 48 rows at least one has length 32.
All inputs are finite; a program needn't handle non-finite values.
Results may differ from the reference program's by a relative error of at most 0.011.
Values may be sent and summed in bfloat16 or wider, within the bound.
No kernel may reach another device: no remote copies, remote signals or barrier semaphores. Data moves between devices by JAX's collectives and lax.ppermute only.
A program may use at most 128 MiB of HBM per device.

```python
import math
import jax
import jax.numpy as jnp
from jax import lax

HEADS = 64
KV_HEADS = 8
HEAD_DIM = 128
OUT_WIN = 4096
RANK = 64
ADP_DEV = 16
ADAPTERS = 512
TOPA = 4
ROW_DEV = 48
ROWS = 1536
CACHE = 32
N_ADAPTER = 32


def shared_keys(key):
    stored = jax.random.truncated_normal(key, -6.0, 6.0, (ROWS, KV_HEADS, CACHE, HEAD_DIM), jnp.float32)
    return stored


def draw_cache_keys(key, part):
    stored = shared_keys(key)
    return stored.astype(jnp.bfloat16)


def draw_queries(key, part):
    key = jax.random.fold_in(key, 3)
    group_size = HEADS // KV_HEADS
    drawn = jax.random.truncated_normal(key, -6.0, 6.0, (ROWS, KV_HEADS, group_size, HEAD_DIM), jnp.float32)
    return drawn.reshape(ROWS, HEADS * HEAD_DIM).astype(jnp.bfloat16)


def draw_new_keys(key, part):
    key = jax.random.fold_in(key, 5)
    drawn = jax.random.truncated_normal(key, -6.0, 6.0, (ROWS, KV_HEADS, HEAD_DIM), jnp.float32)
    return drawn.reshape(ROWS, KV_HEADS * HEAD_DIM).astype(jnp.bfloat16)


def draw_cache_lengths(key, part):
    key = jax.random.fold_in(key, 9)
    first_key, second_key = jax.random.split(key)
    lengths = jax.random.randint(first_key, (N_ADAPTER, ROW_DEV), 1, CACHE + 1)
    longest = jax.random.randint(second_key, (N_ADAPTER,), 0, ROW_DEV)
    lengths = lengths.at[jnp.arange(N_ADAPTER), longest].set(CACHE)
    return lengths.reshape(ROWS).astype(jnp.int32)


def draw_adapter_ids(key, part):
    key = jax.random.fold_in(key, 11)
    busy_key, block_key = jax.random.split(key)
    busiest = jax.random.randint(busy_key, (), 0, N_ADAPTER)
    capacity = ROW_DEV // 2
    pair_count = TOPA * ROW_DEV

    def one_block(inner):
        spread_key, order_key, local_key = jax.random.split(inner, 3)
        picked = jax.random.permutation(spread_key, (N_ADAPTER - 1) * capacity)[:pair_count - capacity]
        others = (busiest + 1 + picked // capacity) % N_ADAPTER
        owners = jnp.concatenate([jnp.full((capacity,), busiest, jnp.int32), others.astype(jnp.int32)])
        owners = owners[jax.random.permutation(order_key, pair_count)]
        scores = jax.random.randint(local_key, (ROW_DEV, ADP_DEV), 0, 2 ** 20) * ADP_DEV + jnp.arange(ADP_DEV)[None, :]
        locals_picked = jnp.argsort(scores, axis=1)[:, :TOPA]
        return owners.reshape(ROW_DEV, TOPA) * ADP_DEV + locals_picked
    block_keys = jax.random.split(block_key, N_ADAPTER)
    return jax.vmap(one_block)(block_keys).reshape(ROWS, TOPA).astype(jnp.int32)


def steps_of(stream_key, dims, pieces, least, largest):
    loudness, own = 1.0, jax.random.fold_in(stream_key, 6)
    for position, blocks in pieces:
        steps = jnp.exp(jax.random.uniform(jax.random.fold_in(own, position), (blocks,), jnp.float32, least / len(pieces), largest / len(pieces)))
        loudness = loudness * jnp.repeat(steps, dims[position] // blocks).reshape([-1 if axis == position else 1 for axis in range(len(dims))])
    return loudness


def scatter_about(rng, extent, scale, bound, shards=(), kind=jnp.bfloat16):
    factor_of = steps_of(rng, extent, shards, -0.22, 0.18) if shards else 1.0
    values = jax.random.normal(rng, extent, jnp.float32) * scale * factor_of
    return jnp.minimum(jnp.maximum(values, -bound), bound).astype(kind)


def setup_inputs(seed: int = 0) -> dict:
    streams_of = jax.random.split(jax.random.key(seed), 12)
    queries = draw_queries(jax.random.fold_in(streams_of[11], 71), 0)
    cache_keys = draw_cache_keys(jax.random.fold_in(streams_of[11], 71), 0)
    cache_values = scatter_about(streams_of[2], (ROWS, KV_HEADS, CACHE, HEAD_DIM), 1.0, 6.0, ((0, 32), (1, 8)))
    new_keys = draw_new_keys(jax.random.fold_in(streams_of[11], 71), 0)
    new_values = scatter_about(streams_of[4], (ROWS, KV_HEADS * HEAD_DIM), 1.0, 6.0, ((0, 32), (1, 8)))
    cache_lengths = draw_cache_lengths(jax.random.fold_in(streams_of[11], 71), 0)
    out_weight = scatter_about(streams_of[6], (HEADS * HEAD_DIM, OUT_WIN), (HEADS * HEAD_DIM) ** -0.5, 0.0625, ((0, 8),))
    adapter_down = scatter_about(streams_of[7], (HEADS * HEAD_DIM, ADAPTERS * RANK), (HEADS * HEAD_DIM) ** -0.5, 0.0625, ((0, 8), (1, 32)))
    adapter_up = scatter_about(streams_of[8], (ADAPTERS * RANK, OUT_WIN), RANK ** -0.5, 0.75, ((0, 32), (1, 8)))
    adapter_ids = draw_adapter_ids(jax.random.fold_in(streams_of[11], 71), 0)
    hub_weights = jnp.clip(jax.random.uniform(streams_of[10], (ROWS, TOPA), jnp.float32, -1.5, 1.5) * steps_of(streams_of[10], (ROWS, TOPA), ((0, 32),), -0.4, 0.0), -1.5, 1.5)
    return {"queries": queries, "cache_keys": cache_keys, "cache_values": cache_values, "new_keys": new_keys, "new_values": new_values, "cache_lengths": cache_lengths, "out_weight": out_weight, "adapter_down": adapter_down, "adapter_up": adapter_up, "adapter_ids": adapter_ids, "hub_weights": hub_weights}


def attend(queries, cache_keys, cache_values, new_keys, new_values, cache_lengths):
    group_size = HEADS // KV_HEADS
    query_heads = queries.astype(jnp.float32).reshape(ROWS, KV_HEADS, group_size, HEAD_DIM)
    scale_factor = 1.0 / math.sqrt(HEAD_DIM)
    cached_scores = jnp.einsum('rkgd,rkld->rkgl', query_heads, cache_keys.astype(jnp.float32), precision=lax.Precision.HIGHEST) * scale_factor
    fresh_keys = new_keys.astype(jnp.float32).reshape(ROWS, KV_HEADS, HEAD_DIM)
    new_scores = jnp.einsum('rkgd,rkd->rkg', query_heads, fresh_keys, precision=lax.Precision.HIGHEST) * scale_factor
    usable = (jnp.arange(CACHE)[None, :] < cache_lengths[:, None])[:, None, None, :]
    cached_scores = jnp.where(usable, cached_scores, -jnp.inf)
    highest = jnp.maximum(lax.optimization_barrier(jnp.max(cached_scores, axis=-1)), new_scores)
    cached_probs = jnp.where(usable, jnp.exp(cached_scores - highest[..., None]), 0.0)
    new_probs = jnp.exp(new_scores - highest)
    totals = lax.optimization_barrier(jnp.sum(cached_probs, axis=-1)) + new_probs
    cached_weights = lax.optimization_barrier(cached_probs.astype(jnp.bfloat16))
    new_weights = lax.optimization_barrier(new_probs.astype(jnp.bfloat16))
    fresh_values = new_values.astype(jnp.float32).reshape(ROWS, KV_HEADS, 1, HEAD_DIM)
    summed = jnp.einsum('rkgl,rkld->rkgd', cached_weights.astype(jnp.float32), cache_values.astype(jnp.float32), precision=lax.Precision.HIGHEST)
    summed = summed + new_weights.astype(jnp.float32)[..., None] * fresh_values
    return (summed / totals[..., None]).astype(jnp.bfloat16).reshape(ROWS, HEADS * HEAD_DIM)

def reference(queries, cache_keys, cache_values, new_keys, new_values, cache_lengths, out_weight, adapter_down, adapter_up, adapter_ids, hub_weights):
    attended = attend(queries, cache_keys, cache_values, new_keys, new_values, cache_lengths)
    frozen = jnp.dot(attended, out_weight, preferred_element_type=jnp.float32)
    down_stack = adapter_down.reshape(HEADS * HEAD_DIM, ADAPTERS, RANK)
    up_stack = adapter_up.reshape(ADAPTERS, RANK, OUT_WIN)

    def one_row(item):
        features, chosen, coefs = item
        down_cols = down_stack[:, chosen, :].astype(jnp.float32)
        lowered = jnp.einsum('f,fjk->jk', features.astype(jnp.float32), down_cols, precision=lax.Precision.HIGHEST)
        mixed = lax.optimization_barrier(jnp.sum(coefs[:, None] * lowered, axis=0)).astype(jnp.bfloat16)
        up_rows = up_stack[chosen].astype(jnp.float32)
        raised = jnp.einsum('k,jko->jo', mixed.astype(jnp.float32), up_rows, precision=lax.Precision.HIGHEST).astype(jnp.bfloat16)
        return lax.optimization_barrier(jnp.sum(coefs[:, None] * raised.astype(jnp.float32), axis=0))
    delta = lax.map(one_row, (attended, adapter_ids, hub_weights))
    return (frozen + delta).astype(jnp.bfloat16)
```

```python
import functools
import math

import jax
import jax.numpy as jnp
from jax import lax
from jax.experimental import pallas as pl
from jax.experimental.pallas import tpu as pltpu
from jax.sharding import PartitionSpec as P

HEADS = 64
KV_HEADS = 8
GROUP = HEADS // KV_HEADS
HEAD_DIM = 128
RANK = 64
ADP_DEV = 16
TOPA = 4
CAP = 24
ROWS = 48
OWNERS = 32
PART = 8
PARTS = CAP // PART
LINES = OWNERS * PART
FEATS = GROUP * HEAD_DIM
COLS = 512
TENSOR = 8
CHUNK = 16
BF = jnp.bfloat16
F32 = jnp.float32


def iota(shape, dim):
    return lax.broadcasted_iota(jnp.int32, shape, dim)


def dot(a, b, contract=((1,), (0,))):
    return lax.dot_general(a, b, (contract, ((), ())), preferred_element_type=F32)


def split_parts(x):
    high = x.astype(BF)
    low = (x - high.astype(F32)).astype(BF)
    return high, low


def attend_kernel(q, ck, cv, nk, nv, lens, ids, hub, att, picks, pay):
    scale = 1.0 / math.sqrt(HEAD_DIM)
    keys = CHUNK * 32
    wide = CHUNK * GROUP
    row_of = iota((wide, keys), 0) & (CHUNK - 1)
    col = iota((wide, keys), 1)
    for c in range(ROWS // CHUNK):
        rows = pl.ds(c * CHUNK, CHUNK)
        qc = q[rows, :]
        qs = jnp.concatenate([qc[:, h * HEAD_DIM : (h + 1) * HEAD_DIM] for h in range(GROUP)], axis=0)
        kc = ck[pl.ds(c * keys, keys), :]
        vc = cv[pl.ds(c * keys, keys), :]
        scores = dot(qs, kc, ((1,), (1,))) * scale
        held = jnp.concatenate([lens[rows, :]] * GROUP, axis=0)
        usable = (row_of == (col >> 5)) & ((col & 31) < held)
        scores = jnp.where(usable, scores, -jnp.inf)
        fresh_k = jnp.concatenate([nk[rows, :].astype(F32)] * GROUP, axis=0)
        fresh_v = jnp.concatenate([nv[rows, :].astype(F32)] * GROUP, axis=0)
        new_scores = jnp.sum(qs.astype(F32) * fresh_k, axis=1, keepdims=True) * scale
        highest = jnp.maximum(jnp.max(scores, axis=1, keepdims=True), new_scores)
        probs = jnp.exp(scores - highest)
        new_probs = jnp.exp(new_scores - highest)
        totals = jnp.sum(probs, axis=1, keepdims=True) + new_probs
        summed = dot(probs.astype(BF), vc) + new_probs.astype(BF).astype(F32) * fresh_v
        out = (summed / totals).astype(BF)
        for h in range(GROUP):
            att[rows, h * HEAD_DIM : (h + 1) * HEAD_DIM] = out[h * CHUNK : (h + 1) * CHUNK, :]

    owner_of_line = iota((ROWS, LINES), 1) >> 3
    named = jnp.zeros((ROWS, LINES), jnp.bool_)
    adapter_of_col = iota((ROWS, OWNERS * ADP_DEV), 1)
    coef = jnp.zeros((ROWS, OWNERS * ADP_DEV), F32)
    for j in range(TOPA):
        idj = ids[:, j : j + 1]
        named = named | ((idj >> 4) == owner_of_line)
        coef = coef + jnp.where(idj == adapter_of_col, hub[:, j : j + 1], 0.0)
    earlier = (iota((ROWS, ROWS), 1) < iota((ROWS, ROWS), 0)).astype(BF)
    place = dot(earlier, named.astype(BF)).astype(jnp.int32)
    place = jnp.where(named, place, -1)
    spot = iota((ROWS, LINES), 1) & (PART - 1)
    high, low = split_parts(coef)
    shape = (LINES, OWNERS * ADP_DEV)
    mine = (iota(shape, 0) >> 3) == (iota(shape, 1) >> 4)
    fold_shape = (OWNERS * ADP_DEV, 128)
    within = iota(fold_shape, 0) & (ADP_DEV - 1)
    lane = iota(fold_shape, 1)
    meta = jnp.zeros((LINES, 128), F32)
    everything = att[...]
    for g in range(PARTS):
        pick = (place == spot + g * PART).astype(BF)
        picks[pl.ds(g * ROWS, ROWS), :] = pick
        pay[:, g * FEATS : (g + 1) * FEATS] = dot(pick, everything, ((0,), (0,))).astype(BF)
        for k, piece in enumerate((high, low)):
            spread = jnp.where(mine, dot(pick, piece, ((0,), (0,))), 0.0).astype(BF)
            fold = (lane == within + (g * 32 + k * ADP_DEV)).astype(BF)
            meta = meta + dot(spread, fold)
    pay[:, PARTS * FEATS :] = meta.astype(BF)


def coefs_of(meta, g):
    shape = (128, ADP_DEV * RANK)
    line = iota(shape, 0)
    adapter = iota(shape, 1) >> 6
    spread = (line == adapter + g * 32) | (line == adapter + (g * 32 + ADP_DEV))
    return dot(meta, spread.astype(BF))


def join_parts(pieces):
    lane = iota((pieces[0].shape[0], 128), 1)
    first = jnp.where(lane < RANK, pieces[0], pieces[1])
    second = jnp.where(lane < RANK, pieces[2], 0.0)
    return jnp.concatenate([first, second], axis=1)


def lower_kernel(got, down, out):
    meta = got[:, PARTS * FEATS :]
    weights = down[...]
    pieces = []
    for g in range(PARTS):
        lowered = dot(got[:, g * FEATS : (g + 1) * FEATS], weights) * coefs_of(meta, g)
        total = lowered[:, :128]
        for p in range(1, ADP_DEV * RANK // 128):
            total = total + lowered[:, p * 128 : (p + 1) * 128]
        pieces.append(total + pltpu.roll(total, RANK, 1))
    out[...] = join_parts(pieces).astype(BF)


def home_kernel(got, picks, out):
    lane = iota((ROWS, 256), 1)
    total = jnp.zeros((ROWS, 256), F32)
    for g in range(PARTS):
        part = dot(picks[pl.ds(g * ROWS, ROWS), :], got[...])
        total = total + jnp.where((lane >> 6) == g, part, 0.0)
    folded = total[:, :128] + total[:, 128:]
    folded = folded + pltpu.roll(folded, RANK, 1)
    for t in range(TENSOR):
        out[pl.ds(t * ROWS, ROWS), :] = folded


def mix_kernel(got, picks, out):
    total = got[pl.ds(0, ROWS), :]
    for t in range(1, TENSOR):
        total = total + got[pl.ds(t * ROWS, ROWS), :]
    mixed = total.astype(BF)
    pieces = [dot(picks[pl.ds(g * ROWS, ROWS), :], mixed, ((0,), (0,))) for g in range(PARTS)]
    out[...] = join_parts(pieces).astype(BF)


def raise_kernel(got, meta, up, out):
    shape = (256, ADP_DEV * RANK)
    line = iota(shape, 0)
    rank = iota(shape, 1) & (RANK - 1)
    for g in range(PARTS):
        tiled = dot(got[...], (line == rank + g * RANK).astype(BF))
        expanded = (tiled * coefs_of(meta[...], g)).astype(BF)
        out[:, g * COLS : (g + 1) * COLS] = dot(expanded, up[...]).astype(BF)


def final_kernel(got, picks, frozen, out):
    total = frozen[...]
    for g in range(PARTS):
        total = total + dot(picks[pl.ds(g * ROWS, ROWS), :], got[:, g * COLS : (g + 1) * COLS])
    out[...] = total.astype(BF)


def call(kernel, out_shape, *args):
    return pl.pallas_call(
        kernel,
        out_shape=out_shape,
        compiler_params=pltpu.CompilerParams(vmem_limit_bytes=48 * 1024 * 1024),
    )(*args)


def shape_of(*shape, dtype=BF):
    return jax.ShapeDtypeStruct(shape, dtype)


def swap(x, axis):
    return lax.all_to_all(x, axis, split_axis=0, concat_axis=0, tiled=True)


def local(
    queries,
    cache_keys,
    cache_values,
    new_keys,
    new_values,
    cache_lengths,
    out_weight,
    adapter_down,
    adapter_up,
    adapter_ids,
    hub_weights,
):
    attended, picks, payload = call(
        attend_kernel,
        (
            shape_of(ROWS, FEATS),
            shape_of(PARTS * ROWS, LINES),
            shape_of(LINES, PARTS * FEATS + 128),
        ),
        queries,
        cache_keys.reshape(-1, HEAD_DIM),
        cache_values.reshape(-1, HEAD_DIM),
        new_keys,
        new_values,
        cache_lengths.reshape(ROWS, 1),
        adapter_ids,
        hub_weights,
    )
    got = swap(payload, "adapter")
    frozen_part = jnp.dot(attended, out_weight, preferred_element_type=F32)
    got, frozen_part = lax.optimization_barrier((got, frozen_part))
    frozen = lax.psum_scatter(frozen_part, "tensor", scatter_dimension=1, tiled=True)
    lowered = call(lower_kernel, shape_of(LINES, 256), got, adapter_down)
    lowered = swap(lowered, "adapter")
    share = call(home_kernel, shape_of(TENSOR * ROWS, 128, dtype=F32), lowered, picks)
    share = swap(share, "tensor")
    mixed = call(mix_kernel, shape_of(LINES, 256), share, picks)
    mixed = swap(mixed, "adapter")
    meta = got[:, PARTS * FEATS :]
    raised = call(raise_kernel, shape_of(LINES, PARTS * COLS), mixed, meta, adapter_up)
    raised = swap(raised, "adapter")
    return call(final_kernel, shape_of(ROWS, COLS), raised, picks, frozen)


def solution(mesh):
    return jax.shard_map(
        local,
        mesh=mesh,
        in_specs=(
            P("adapter", "tensor"),
            P("adapter", "tensor", None, None),
            P("adapter", "tensor", None, None),
            P("adapter", "tensor"),
            P("adapter", "tensor"),
            P("adapter"),
            P("tensor", None),
            P("tensor", "adapter"),
            P("adapter", "tensor"),
            P("adapter", None),
            P("adapter", None),
        ),
        out_specs=P("adapter", "tensor"),
        check_vma=False,
    )
```

```python
import functools
import math

import jax
import jax.numpy as jnp
from jax import lax
from jax.experimental import pallas as pl
from jax.experimental.pallas import tpu as pltpu
from jax.sharding import PartitionSpec as P

HEADS = 64
KV_HEADS = 8
GROUP = HEADS // KV_HEADS
HEAD_DIM = 128
RANK = 64
ADP_DEV = 16
TOPA = 4
CAP = 24
ROWS = 48
OWNERS = 32
PART = 8
PARTS = CAP // PART
LINES = OWNERS * PART
FEATS = GROUP * HEAD_DIM
COLS = 512
TENSOR = 8
CORES = 2
CHIPS = 4
DOWN_STEPS = 4
CHUNK = 16
BF = jnp.bfloat16
F32 = jnp.float32


def iota(shape, dim):
    return lax.broadcasted_iota(jnp.int32, shape, dim)


def dot(a, b, contract=((1,), (0,))):
    return lax.dot_general(a, b, (contract, ((), ())), preferred_element_type=F32)


def split_parts(x):
    high = x.astype(BF)
    low = (x - high.astype(F32)).astype(BF)
    return high, low


def attend_kernel(
    q_hbm, ck_hbm, cv_hbm, nk_hbm, nv_hbm, lens_hbm, ids_hbm, hub_hbm,
    att, picks, pay,
    q, ck, cv, nk, nv, lens, ids, hub, sems,
):
    copies = []
    sources = (ids_hbm, hub_hbm, lens_hbm, q_hbm, ck_hbm, nk_hbm, nv_hbm, cv_hbm)
    for n, (src, dst) in enumerate(zip(sources, (ids, hub, lens, q, ck, nk, nv, cv))):
        copies.append(pltpu.make_async_copy(src, dst, sems.at[n]))
        copies[-1].start()

    diagonal = iota((ROWS, ROWS), 0) == iota((ROWS, ROWS), 1)

    def column(line):
        return jnp.sum(jnp.where(diagonal, line, 0.0), axis=1, keepdims=True)

    copies[0].wait()
    copies[1].wait()
    owner_of_line = iota((ROWS, LINES), 1) >> 3
    named = jnp.zeros((ROWS, LINES), jnp.bool_)
    adapter_of_col = iota((ROWS, OWNERS * ADP_DEV), 1)
    coef = jnp.zeros((ROWS, OWNERS * ADP_DEV), F32)
    for j in range(TOPA):
        idj = column(ids[j : j + 1, :].astype(F32)).astype(jnp.int32)
        named = named | ((idj >> 4) == owner_of_line)
        coef = coef + jnp.where(idj == adapter_of_col, column(hub[j : j + 1, :]), 0.0)
    earlier = (iota((ROWS, ROWS), 1) < iota((ROWS, ROWS), 0)).astype(BF)
    place = dot(earlier, named.astype(BF)).astype(jnp.int32)
    place = jnp.where(named, place, -1)
    spot = iota((ROWS, LINES), 1) & (PART - 1)
    high, low = split_parts(coef)
    shape = (LINES, OWNERS * ADP_DEV)
    mine = (iota(shape, 0) >> 3) == (iota(shape, 1) >> 4)
    fold_shape = (OWNERS * ADP_DEV, 128)
    within = iota(fold_shape, 0) & (ADP_DEV - 1)
    lane = iota(fold_shape, 1)
    meta = jnp.zeros((LINES, 128), F32)
    for g in range(PARTS):
        pick = (place == spot + g * PART).astype(BF)
        picks[pl.ds(g * ROWS, ROWS), :] = pick
        for k, piece in enumerate((high, low)):
            spread = jnp.where(mine, dot(pick, piece, ((0,), (0,))), 0.0).astype(BF)
            fold = (lane == within + (g * 32 + k * ADP_DEV)).astype(BF)
            meta = meta + dot(spread, fold)
    pay[:, PARTS * FEATS :] = meta.astype(BF)

    for copy in copies[2:]:
        copy.wait()
    lengths = column(lens[...].astype(F32)).astype(jnp.int32)
    scale = 1.0 / math.sqrt(HEAD_DIM)
    keys = CHUNK * 32
    wide = CHUNK * GROUP
    row_of = iota((wide, keys), 0) & (CHUNK - 1)
    col = iota((wide, keys), 1)
    for c in range(ROWS // CHUNK):
        rows = pl.ds(c * CHUNK, CHUNK)
        qc = q[rows, :]
        qs = jnp.concatenate([qc[:, h * HEAD_DIM : (h + 1) * HEAD_DIM] for h in range(GROUP)], axis=0)
        kc = ck[pl.ds(c * keys, keys), :]
        vc = cv[pl.ds(c * keys, keys), :]
        scores = dot(qs, kc, ((1,), (1,))) * scale
        held = jnp.concatenate([lengths[c * CHUNK : (c + 1) * CHUNK, :]] * GROUP, axis=0)
        usable = (row_of == (col >> 5)) & ((col & 31) < held)
        scores = jnp.where(usable, scores, -jnp.inf)
        fresh_k = jnp.concatenate([nk[rows, :].astype(F32)] * GROUP, axis=0)
        fresh_v = jnp.concatenate([nv[rows, :].astype(F32)] * GROUP, axis=0)
        new_scores = jnp.sum(qs.astype(F32) * fresh_k, axis=1, keepdims=True) * scale
        highest = jnp.maximum(jnp.max(scores, axis=1, keepdims=True), new_scores)
        probs = jnp.exp(scores - highest)
        new_probs = jnp.exp(new_scores - highest)
        totals = jnp.sum(probs, axis=1, keepdims=True) + new_probs
        summed = dot(probs.astype(BF), vc) + new_probs.astype(BF).astype(F32) * fresh_v
        out = (summed / totals).astype(BF)
        for h in range(GROUP):
            att[rows, h * HEAD_DIM : (h + 1) * HEAD_DIM] = out[h * CHUNK : (h + 1) * CHUNK, :]
    everything = att[...]
    for g in range(PARTS):
        pick = picks[pl.ds(g * ROWS, ROWS), :]
        pay[:, g * FEATS : (g + 1) * FEATS] = dot(pick, everything, ((0,), (0,))).astype(BF)


def coefs_of(meta, g, first=0, count=ADP_DEV):
    shape = (128, count * RANK)
    line = iota(shape, 0)
    adapter = (iota(shape, 1) >> 6) + first
    spread = (line == adapter + g * 32) | (line == adapter + (g * 32 + ADP_DEV))
    return dot(meta, spread.astype(BF))


def join_parts(pieces):
    lane = iota((pieces[0].shape[0], 128), 1)
    first = jnp.where(lane < RANK, pieces[0], pieces[1])
    second = jnp.where(lane < RANK, pieces[2], 0.0)
    return jnp.concatenate([first, second], axis=1)


def lower_kernel(got, down, out, weights, sems):
    width = down.shape[1] // DOWN_STEPS
    held = ADP_DEV // DOWN_STEPS
    copies = []
    for n in range(DOWN_STEPS):
        cols = pl.ds(n * width, width)
        copies.append(pltpu.make_async_copy(down.at[:, cols], weights.at[:, cols], sems.at[n]))
        copies[-1].start()
    meta = got[:, PARTS * FEATS :]
    totals = [jnp.zeros((LINES, 128), F32)] * PARTS
    for n in range(DOWN_STEPS):
        copies[n].wait()
        for g in range(PARTS):
            lowered = dot(got[:, g * FEATS : (g + 1) * FEATS], weights[:, n * width : (n + 1) * width])
            lowered = lowered * coefs_of(meta, g, n * held, held)
            for p in range(width // 128):
                totals[g] = totals[g] + lowered[:, p * 128 : (p + 1) * 128]
    pieces = [total + pltpu.roll(total, RANK, 1) for total in totals]
    out[...] = join_parts(pieces).astype(BF)


def home_kernel(got, picks, out):
    lane = iota((ROWS, 256), 1)
    total = jnp.zeros((ROWS, 256), F32)
    for g in range(PARTS):
        part = dot(picks[pl.ds(g * ROWS, ROWS), :], got[...])
        total = total + jnp.where((lane >> 6) == g, part, 0.0)
    folded = total[:, :128] + total[:, 128:]
    folded = folded + pltpu.roll(folded, RANK, 1)
    half = ROWS // 2
    lane = iota((half, 128), 1)
    packed = jnp.where(lane < RANK, folded[:half, :], folded[half:, :])
    for t in range(TENSOR):
        out[pl.ds(t * half, half), :] = packed


def mix_kernel(got, picks, out):
    half = ROWS // 2
    total = got[pl.ds(0, half), :]
    for t in range(1, TENSOR):
        total = total + got[pl.ds(t * half, half), :]
    other = pltpu.roll(total, RANK, 1)
    lane = iota((half, 128), 1)
    first = jnp.where(lane < RANK, total, other)
    second = jnp.where(lane < RANK, other, total)
    mixed = jnp.concatenate([first, second], axis=0).astype(BF)
    pieces = [dot(picks[pl.ds(g * ROWS, ROWS), :], mixed, ((0,), (0,))) for g in range(PARTS)]
    out[...] = join_parts(pieces).astype(BF)


def raise_kernel(got, meta, up, out):
    shape = (256, ADP_DEV * RANK)
    line = iota(shape, 0)
    rank = iota(shape, 1) & (RANK - 1)
    for g in range(PARTS):
        tiled = dot(got[...], (line == rank + g * RANK).astype(BF))
        expanded = (tiled * coefs_of(meta[...], g)).astype(BF)
        out[:, g * COLS : (g + 1) * COLS] = dot(expanded, up[...]).astype(BF)


def final_kernel(got, picks, frozen, out):
    total = frozen[...]
    for g in range(PARTS):
        total = total + dot(picks[pl.ds(g * ROWS, ROWS), :], got[:, g * COLS : (g + 1) * COLS])
    out[...] = total.astype(BF)


def attend(*args):
    return pl.pallas_call(
        attend_kernel,
        out_shape=(
            shape_of(ROWS, FEATS),
            shape_of(PARTS * ROWS, LINES),
            shape_of(LINES, PARTS * FEATS + 128),
        ),
        in_specs=[pl.BlockSpec(memory_space=pltpu.HBM)] * len(args),
        scratch_shapes=[pltpu.VMEM(x.shape, x.dtype) for x in args]
        + [pltpu.SemaphoreType.DMA((len(args),))],
        compiler_params=pltpu.CompilerParams(vmem_limit_bytes=32 * 1024 * 1024),
    )(*[pltpu.with_memory_space_constraint(x, pltpu.HBM) for x in args])


def lower(got, down):
    return pl.pallas_call(
        lower_kernel,
        out_shape=shape_of(LINES, 256),
        in_specs=[pl.BlockSpec(memory_space=pltpu.VMEM), pl.BlockSpec(memory_space=pltpu.HBM)],
        scratch_shapes=[
            pltpu.VMEM(down.shape, down.dtype),
            pltpu.SemaphoreType.DMA((DOWN_STEPS,)),
        ],
        compiler_params=pltpu.CompilerParams(vmem_limit_bytes=24 * 1024 * 1024),
    )(got, pltpu.with_memory_space_constraint(down, pltpu.HBM))


def call(kernel, out_shape, *args):
    return pl.pallas_call(
        kernel,
        out_shape=out_shape,
        compiler_params=pltpu.CompilerParams(vmem_limit_bytes=24 * 1024 * 1024),
    )(*args)


def shape_of(*shape, dtype=BF):
    return jax.ShapeDtypeStruct(shape, dtype)


def swap(x, axis):
    return lax.all_to_all(x, axis, split_axis=0, concat_axis=0, tiled=True)


def frozen_sum(attended, out_weight):
    index = lax.axis_index("tensor")
    chip, core = index // CORES, index % CORES
    part = jnp.dot(attended, out_weight, preferred_element_type=F32)
    part = part.reshape(ROWS, CHIPS, CORES, COLS)
    kept = jnp.where(core == 0, part[:, :, 0], part[:, :, 1])
    sent = jnp.where(core == 0, part[:, :, 1], part[:, :, 0]).astype(BF)
    came = lax.ppermute(sent, "tensor", [(i, i ^ 1) for i in range(TENSOR)])
    pair = (kept + came.astype(F32)).reshape(ROWS, CHIPS * COLS)
    rounded = pair.astype(BF)
    total = lax.dynamic_slice_in_dim(pair, chip * COLS, COLS, 1)
    for step in range(1, CHIPS):
        block = lax.dynamic_slice_in_dim(rounded, ((chip + step) % CHIPS) * COLS, COLS, 1)
        pairs = [(i, (i + step * CORES) % TENSOR) for i in range(TENSOR)]
        total = total + lax.ppermute(block, "tensor", pairs).astype(F32)
    return total


def local(
    queries,
    cache_keys,
    cache_values,
    new_keys,
    new_values,
    cache_lengths,
    out_weight,
    adapter_down,
    adapter_up,
    adapter_ids,
    hub_weights,
):
    attended, picks, payload = attend(
        queries,
        cache_keys.reshape(-1, HEAD_DIM),
        cache_values.reshape(-1, HEAD_DIM),
        new_keys,
        new_values,
        cache_lengths.reshape(1, ROWS),
        adapter_ids.T,
        hub_weights.T,
    )
    got = swap(payload, "adapter")
    frozen = frozen_sum(attended, out_weight)
    got, frozen = lax.optimization_barrier((got, frozen))
    lowered = lower(got, adapter_down)
    lowered = swap(lowered, "adapter")
    share = call(home_kernel, shape_of(TENSOR * ROWS // 2, 128, dtype=F32), lowered, picks)
    share = swap(share, "tensor")
    mixed = call(mix_kernel, shape_of(LINES, 256), share, picks)
    mixed = swap(mixed, "adapter")
    meta = got[:, PARTS * FEATS :]
    raised = call(raise_kernel, shape_of(LINES, PARTS * COLS), mixed, meta, adapter_up)
    raised = swap(raised, "adapter")
    return call(final_kernel, shape_of(ROWS, COLS), raised, picks, frozen)


def solution(mesh):
    return jax.shard_map(
        local,
        mesh=mesh,
        in_specs=(
            P("adapter", "tensor"),
            P("adapter", "tensor", None, None),
            P("adapter", "tensor", None, None),
            P("adapter", "tensor"),
            P("adapter", "tensor"),
            P("adapter"),
            P("tensor", None),
            P("tensor", "adapter"),
            P("adapter", "tensor"),
            P("adapter", None),
            P("adapter", None),
        ),
        out_specs=P("adapter", "tensor"),
        check_vma=False,
    )
```

```python
import functools
import math

import jax
import jax.numpy as jnp
from jax import lax
from jax.experimental import pallas as pl
from jax.experimental.pallas import tpu as pltpu
from jax.sharding import PartitionSpec as P

HEADS = 64
KV_HEADS = 8
GROUP = HEADS // KV_HEADS
HEAD_DIM = 128
RANK = 64
ADP_DEV = 16
TOPA = 4
CAP = 24
ROWS = 48
OWNERS = 32
PART = 8
PARTS = CAP // PART
LINES = OWNERS * PART
FEATS = GROUP * HEAD_DIM
COLS = 512
TENSOR = 8
CORES = 2
CHIPS = 4
DOWN_STEPS = 4
CHUNK = 16
BF = jnp.bfloat16
F32 = jnp.float32


def iota(shape, dim):
    return lax.broadcasted_iota(jnp.int32, shape, dim)


def dot(a, b, contract=((1,), (0,))):
    return lax.dot_general(a, b, (contract, ((), ())), preferred_element_type=F32)


def column(line):
    diagonal = iota((ROWS, ROWS), 0) == iota((ROWS, ROWS), 1)
    return jnp.sum(jnp.where(diagonal, line, 0.0), axis=1, keepdims=True)


def split_parts(x):
    high = x.astype(BF)
    low = (x - high.astype(F32)).astype(BF)
    return high, low


def attend_kernel(
    q_hbm, ck_hbm, cv_hbm, nk_hbm, nv_hbm, lens_hbm, ids_hbm, hub_hbm,
    att, picks, pay,
    q, ck, cv, nk, nv, lens, ids, hub, sems, made, out_sems,
):
    def leave(g, start, width):
        cols = pl.ds(start, width)
        copy = pltpu.make_async_copy(made.at[:, cols], pay.at[:, cols], out_sems.at[g])
        copy.start()
        return copy

    copies = []
    sources = (ids_hbm, hub_hbm, lens_hbm, q_hbm, ck_hbm, nk_hbm, nv_hbm, cv_hbm)
    for n, (src, dst) in enumerate(zip(sources, (ids, hub, lens, q, ck, nk, nv, cv))):
        copies.append(pltpu.make_async_copy(src, dst, sems.at[n]))
        copies[-1].start()

    copies[0].wait()
    copies[1].wait()
    shape = (LINES, ROWS)
    owner_of_line = iota(shape, 0) >> 3
    hits = [(ids[j : j + 1, :] >> 4) == owner_of_line for j in range(TOPA)]
    named = (hits[0] | hits[1]) | (hits[2] | hits[3])
    earlier = (iota((ROWS, ROWS), 0) < iota((ROWS, ROWS), 1)).astype(BF)
    place = dot(named.astype(BF), earlier).astype(jnp.int32)
    place = jnp.where(named, place, -1)
    spot = iota(shape, 0) & (PART - 1)
    line = iota((128, ROWS), 0)
    spreads = []
    for j in range(TOPA):
        within = ids[j : j + 1, :] & (ADP_DEV - 1)
        high, low = split_parts(hub[j : j + 1, :])
        spread = jnp.where(line == within, high.astype(F32), 0.0)
        spread = jnp.where(line == within + ADP_DEV, low.astype(F32), spread)
        spreads.append(spread.astype(BF))
    meta = jnp.zeros((LINES, 128), F32)
    for g in range(PARTS):
        pick = place == spot + g * PART
        picks[pl.ds(g * LINES, LINES), :] = pick.astype(BF)
        coefs = jnp.zeros((LINES, 128), F32)
        for j in range(TOPA):
            coefs = coefs + dot((pick & hits[j]).astype(BF), spreads[j], ((1,), (1,)))
        meta = meta + (pltpu.roll(coefs, g * 2 * ADP_DEV, 1) if g else coefs)
    made[:, PARTS * FEATS :] = meta.astype(BF)
    leaving = [leave(PARTS, PARTS * FEATS, 128)]

    for copy in copies[2:]:
        copy.wait()
    lengths = column(lens[...].astype(F32)).astype(jnp.int32)
    scale = 1.0 / math.sqrt(HEAD_DIM)
    keys = CHUNK * 32
    wide = CHUNK * GROUP
    row_of = iota((wide, keys), 0) & (CHUNK - 1)
    col = iota((wide, keys), 1)
    for c in range(ROWS // CHUNK):
        rows = pl.ds(c * CHUNK, CHUNK)
        qc = q[rows, :]
        qs = jnp.concatenate([qc[:, h * HEAD_DIM : (h + 1) * HEAD_DIM] for h in range(GROUP)], axis=0)
        kc = ck[pl.ds(c * keys, keys), :]
        vc = cv[pl.ds(c * keys, keys), :]
        scores = dot(qs, kc, ((1,), (1,))) * scale
        held = jnp.concatenate([lengths[c * CHUNK : (c + 1) * CHUNK, :]] * GROUP, axis=0)
        usable = (row_of == (col >> 5)) & ((col & 31) < held)
        scores = jnp.where(usable, scores, -jnp.inf)
        fresh_k = jnp.concatenate([nk[rows, :].astype(F32)] * GROUP, axis=0)
        fresh_v = jnp.concatenate([nv[rows, :].astype(F32)] * GROUP, axis=0)
        new_scores = jnp.sum(qs.astype(F32) * fresh_k, axis=1, keepdims=True) * scale
        highest = jnp.maximum(jnp.max(scores, axis=1, keepdims=True), new_scores)
        probs = jnp.exp(scores - highest)
        new_probs = jnp.exp(new_scores - highest)
        totals = jnp.sum(probs, axis=1, keepdims=True) + new_probs
        summed = dot(probs.astype(BF), vc) + new_probs.astype(BF).astype(F32) * fresh_v
        out = (summed / totals).astype(BF)
        for h in range(GROUP):
            att[rows, h * HEAD_DIM : (h + 1) * HEAD_DIM] = out[h * CHUNK : (h + 1) * CHUNK, :]
    everything = att[...]
    for g in range(PARTS):
        pick = picks[pl.ds(g * LINES, LINES), :]
        made[:, g * FEATS : (g + 1) * FEATS] = dot(pick, everything).astype(BF)
        leaving.append(leave(g, g * FEATS, FEATS))
    for copy in leaving:
        copy.wait()


def coefs_of(meta, g, first=0, count=ADP_DEV):
    shape = (128, count * RANK)
    line = iota(shape, 0)
    adapter = (iota(shape, 1) >> 6) + first
    spread = (line == adapter + g * 32) | (line == adapter + (g * 32 + ADP_DEV))
    return dot(meta, spread.astype(BF))


def join_parts(pieces):
    lane = iota((pieces[0].shape[0], 128), 1)
    first = jnp.where(lane < RANK, pieces[0], pieces[1])
    second = jnp.where(lane < RANK, pieces[2], 0.0)
    return jnp.concatenate([first, second], axis=1)


def lower_kernel(got, down, out, weights, sems):
    width = down.shape[1] // DOWN_STEPS
    copies = []
    for n in range(DOWN_STEPS):
        cols = pl.ds(n * width, width)
        copies.append(pltpu.make_async_copy(down.at[:, cols], weights.at[:, cols], sems.at[n]))
        copies[-1].start()
    meta = got[:, PARTS * FEATS :]
    coefs = [coefs_of(meta, g) for g in range(PARTS)]
    totals = [jnp.zeros((LINES, 128), F32)] * PARTS
    for n in range(DOWN_STEPS):
        copies[n].wait()
        block = weights[:, n * width : (n + 1) * width]
        for g in range(PARTS):
            lowered = dot(got[:, g * FEATS : (g + 1) * FEATS], block)
            lowered = lowered * coefs[g][:, n * width : (n + 1) * width]
            for p in range(width // 128):
                totals[g] = totals[g] + lowered[:, p * 128 : (p + 1) * 128]
    pieces = [total + pltpu.roll(total, RANK, 1) for total in totals]
    out[...] = join_parts(pieces).astype(BF)


def pick_kernel(ids, after, picks):
    owner_of_line = iota((ROWS, LINES), 1) >> 3
    named = jnp.zeros((ROWS, LINES), jnp.bool_)
    for j in range(TOPA):
        owner = column(ids[j : j + 1, :].astype(F32)).astype(jnp.int32) >> 4
        named = named | (owner == owner_of_line)
    earlier = (iota((ROWS, ROWS), 1) < iota((ROWS, ROWS), 0)).astype(BF)
    place = dot(earlier, named.astype(BF)).astype(jnp.int32)
    place = jnp.where(named, place, -1)
    spot = iota((ROWS, LINES), 1) & (PART - 1)
    for g in range(PARTS):
        picks[pl.ds(g * ROWS, ROWS), :] = (place == spot + g * PART).astype(BF)


def home_kernel(got, picks, out):
    lane = iota((ROWS, 256), 1)
    total = jnp.zeros((ROWS, 256), F32)
    for g in range(PARTS):
        part = dot(picks[pl.ds(g * ROWS, ROWS), :], got[...])
        total = total + jnp.where((lane >> 6) == g, part, 0.0)
    folded = total[:, :128] + total[:, 128:]
    folded = folded + pltpu.roll(folded, RANK, 1)
    half = ROWS // 2
    lane = iota((half, 128), 1)
    out[...] = jnp.where(lane < RANK, folded[:half, :], folded[half:, :])


def mix_kernel(own, ahead, behind, across, picks, out):
    half = ROWS // 2
    total = (own[...] + ahead[...]) + (behind[...] + across[...])
    other = pltpu.roll(total, RANK, 1)
    lane = iota((half, 128), 1)
    first = jnp.where(lane < RANK, total, other)
    second = jnp.where(lane < RANK, other, total)
    mixed = jnp.concatenate([first, second], axis=0).astype(BF)
    pieces = [dot(picks[pl.ds(g * LINES, LINES), :], mixed) for g in range(PARTS)]
    out[...] = join_parts(pieces).astype(BF)


def raise_kernel(got, meta, up, out):
    lane = iota((LINES, 128), 1)
    first = got[:, :128].astype(F32)
    second = got[:, 128:].astype(F32)
    turned = pltpu.roll(first, RANK, 1)
    pairs = (
        jnp.where(lane < RANK, first, turned),
        jnp.where(lane < RANK, turned, first),
        jnp.where(lane < RANK, second, pltpu.roll(second, RANK, 1)),
    )
    blocks = []
    for g in range(PARTS):
        coefs = coefs_of(meta[...], g)
        blocks.append(
            jnp.concatenate(
                [
                    (coefs[:, p * 128 : (p + 1) * 128] * pairs[g]).astype(BF)
                    for p in range(ADP_DEV * RANK // 128)
                ],
                axis=1,
            )
        )
    raised = dot(jnp.concatenate(blocks, axis=0), up[...]).astype(BF)
    for g in range(PARTS):
        out[:, g * COLS : (g + 1) * COLS] = raised[g * LINES : (g + 1) * LINES, :]


def final_kernel(got, picks, frozen, out):
    total = frozen[...]
    for g in range(PARTS):
        total = total + dot(picks[pl.ds(g * ROWS, ROWS), :], got[:, g * COLS : (g + 1) * COLS])
    out[...] = total.astype(BF)


def attend(*args):
    return pl.pallas_call(
        attend_kernel,
        out_shape=(
            shape_of(ROWS, FEATS),
            shape_of(PARTS * LINES, ROWS),
            shape_of(LINES, PARTS * FEATS + 128),
        ),
        in_specs=[pl.BlockSpec(memory_space=pltpu.HBM)] * len(args),
        out_specs=(
            pl.BlockSpec(memory_space=pltpu.VMEM),
            pl.BlockSpec(memory_space=pltpu.VMEM),
            pl.BlockSpec(memory_space=pltpu.HBM),
        ),
        scratch_shapes=[pltpu.VMEM(x.shape, x.dtype) for x in args]
        + [
            pltpu.SemaphoreType.DMA((len(args),)),
            pltpu.VMEM((LINES, PARTS * FEATS + 128), BF),
            pltpu.SemaphoreType.DMA((PARTS + 1,)),
        ],
        compiler_params=pltpu.CompilerParams(vmem_limit_bytes=32 * 1024 * 1024),
    )(*[pltpu.with_memory_space_constraint(x, pltpu.HBM) for x in args])


def lower(got, down):
    return pl.pallas_call(
        lower_kernel,
        out_shape=shape_of(LINES, 256),
        in_specs=[pl.BlockSpec(memory_space=pltpu.VMEM), pl.BlockSpec(memory_space=pltpu.HBM)],
        scratch_shapes=[
            pltpu.VMEM(down.shape, down.dtype),
            pltpu.SemaphoreType.DMA((DOWN_STEPS,)),
        ],
        compiler_params=pltpu.CompilerParams(vmem_limit_bytes=24 * 1024 * 1024),
    )(got, pltpu.with_memory_space_constraint(down, pltpu.HBM))


def call(kernel, out_shape, *args):
    return pl.pallas_call(
        kernel,
        out_shape=out_shape,
        compiler_params=pltpu.CompilerParams(vmem_limit_bytes=24 * 1024 * 1024),
    )(*args)


def shape_of(*shape, dtype=BF):
    return jax.ShapeDtypeStruct(shape, dtype)


def swap(x, axis):
    return lax.all_to_all(x, axis, split_axis=0, concat_axis=0, tiled=True)


def turn(x, chips, cores):
    pairs = [
        (i, (i // CORES + chips) % CHIPS * CORES + (i + cores) % CORES) for i in range(TENSOR)
    ]
    return lax.ppermute(x, "tensor", pairs)


def frozen_sum(attended, out_weight):
    index = lax.axis_index("tensor")
    chip, core = index // CORES, index % CORES
    part = jnp.dot(attended, out_weight, preferred_element_type=F32)
    part = part.reshape(ROWS, CHIPS, CORES, COLS)
    kept = jnp.where(core == 0, part[:, :, 0], part[:, :, 1])
    sent = jnp.where(core == 0, part[:, :, 1], part[:, :, 0]).astype(BF)
    came = turn(sent, 0, 1)
    pair = (kept + came.astype(F32)).reshape(ROWS, CHIPS * COLS)
    rounded = pair.astype(BF)
    total = lax.dynamic_slice_in_dim(pair, chip * COLS, COLS, 1)
    for step in range(1, CHIPS):
        block = lax.dynamic_slice_in_dim(rounded, ((chip + step) % CHIPS) * COLS, COLS, 1)
        total = total + turn(block, step, 0).astype(F32)
    return total


def local(
    queries,
    cache_keys,
    cache_values,
    new_keys,
    new_values,
    cache_lengths,
    out_weight,
    adapter_down,
    adapter_up,
    adapter_ids,
    hub_weights,
):
    attended, picks_out, payload = attend(
        queries,
        cache_keys.reshape(-1, HEAD_DIM),
        cache_values.reshape(-1, HEAD_DIM),
        new_keys,
        new_values,
        cache_lengths.reshape(1, ROWS),
        adapter_ids.T,
        hub_weights.T,
    )
    got = swap(payload, "adapter")
    frozen = frozen_sum(attended, out_weight)
    picks = call(pick_kernel, shape_of(PARTS * ROWS, LINES), adapter_ids.T, attended)
    got, frozen, picks = lax.optimization_barrier((got, frozen, picks))
    lowered = lower(got, adapter_down)
    lowered = swap(lowered, "adapter")
    share = call(home_kernel, shape_of(ROWS // 2, 128, dtype=F32), lowered, picks)
    share = share + turn(share, 0, 1)
    shares = [turn(share, step, 0) for step in (1, CHIPS - 1, 2)]
    mixed = call(mix_kernel, shape_of(LINES, 256), share, *shares, picks_out)
    mixed = swap(mixed, "adapter")
    meta = got[:, PARTS * FEATS :]
    raised = call(raise_kernel, shape_of(LINES, PARTS * COLS), mixed, meta, adapter_up)
    raised = swap(raised, "adapter")
    return call(final_kernel, shape_of(ROWS, COLS), raised, picks, frozen)


def solution(mesh):
    return jax.shard_map(
        local,
        mesh=mesh,
        in_specs=(
            P("adapter", "tensor"),
            P("adapter", "tensor", None, None),
            P("adapter", "tensor", None, None),
            P("adapter", "tensor"),
            P("adapter", "tensor"),
            P("adapter"),
            P("tensor", None),
            P("tensor", "adapter"),
            P("adapter", "tensor"),
            P("adapter", None),
            P("adapter", None),
        ),
        out_specs=P("adapter", "tensor"),
        check_vma=False,
    )
```

```python
import functools
import math

import jax
import jax.numpy as jnp
from jax import lax
from jax.experimental import pallas as pl
from jax.experimental.pallas import tpu as pltpu
from jax.sharding import PartitionSpec as P

HEADS = 64
KV_HEADS = 8
GROUP = HEADS // KV_HEADS
HEAD_DIM = 128
RANK = 64
ADP_DEV = 16
TOPA = 4
CAP = 24
ROWS = 48
OWNERS = 32
PART = 8
PARTS = CAP // PART
LINES = OWNERS * PART
FEATS = GROUP * HEAD_DIM
COLS = 512
TENSOR = 8
CORES = 2
CHIPS = 4
DOWN_STEPS = 4
DEPTH = 8
SIDES = 4
COLUMNS = [[y * DEPTH + z for z in range(DEPTH)] for y in range(SIDES)]
CHUNK = 16
BF = jnp.bfloat16
F32 = jnp.float32


def iota(shape, dim):
    return lax.broadcasted_iota(jnp.int32, shape, dim)


def dot(a, b, contract=((1,), (0,))):
    return lax.dot_general(a, b, (contract, ((), ())), preferred_element_type=F32)


def column(line):
    diagonal = iota((ROWS, ROWS), 0) == iota((ROWS, ROWS), 1)
    return jnp.sum(jnp.where(diagonal, line, 0.0), axis=1, keepdims=True)


def split_parts(x):
    high = x.astype(BF)
    low = (x - high.astype(F32)).astype(BF)
    return high, low


def attend_kernel(
    q_hbm, ck_hbm, cv_hbm, nk_hbm, nv_hbm, lens_hbm, ids_hbm, hub_hbm,
    att, pay,
    picks, q, ck, cv, nk, nv, lens, ids, hub, sems, made, out_sems,
):
    def leave(g, start, width):
        cols = pl.ds(start, width)
        copy = pltpu.make_async_copy(made.at[:, cols], pay.at[:, cols], out_sems.at[g])
        copy.start()
        return copy

    copies = []
    sources = (ids_hbm, hub_hbm, lens_hbm, q_hbm, ck_hbm, nk_hbm, nv_hbm, cv_hbm)
    for n, (src, dst) in enumerate(zip(sources, (ids, hub, lens, q, ck, nk, nv, cv))):
        copies.append(pltpu.make_async_copy(src, dst, sems.at[n]))
        copies[-1].start()

    copies[0].wait()
    copies[1].wait()
    shape = (LINES, ROWS)
    owner_of_line = iota(shape, 0) >> 3
    hits = [(ids[j : j + 1, :] >> 4) == owner_of_line for j in range(TOPA)]
    named = (hits[0] | hits[1]) | (hits[2] | hits[3])
    earlier = (iota((ROWS, ROWS), 0) < iota((ROWS, ROWS), 1)).astype(BF)
    place = dot(named.astype(BF), earlier).astype(jnp.int32)
    place = jnp.where(named, place, -1)
    spot = iota(shape, 0) & (PART - 1)
    line = iota((128, ROWS), 0)
    spreads = []
    for j in range(TOPA):
        within = ids[j : j + 1, :] & (ADP_DEV - 1)
        high, low = split_parts(hub[j : j + 1, :])
        spread = jnp.where(line == within, high.astype(F32), 0.0)
        spread = jnp.where(line == within + ADP_DEV, low.astype(F32), spread)
        spreads.append(spread.astype(BF))
    meta = jnp.zeros((LINES, 128), F32)
    for g in range(PARTS):
        pick = place == spot + g * PART
        picks[pl.ds(g * LINES, LINES), :] = pick.astype(BF)
        coefs = jnp.zeros((LINES, 128), F32)
        for j in range(TOPA):
            coefs = coefs + dot((pick & hits[j]).astype(BF), spreads[j], ((1,), (1,)))
        meta = meta + (pltpu.roll(coefs, g * 2 * ADP_DEV, 1) if g else coefs)
    made[:, PARTS * FEATS :] = meta.astype(BF)
    leaving = [leave(PARTS, PARTS * FEATS, 128)]

    for copy in copies[2:]:
        copy.wait()
    lengths = column(lens[...].astype(F32)).astype(jnp.int32)
    scale = 1.0 / math.sqrt(HEAD_DIM)
    keys = CHUNK * 32
    wide = CHUNK * GROUP
    row_of = iota((wide, keys), 0) & (CHUNK - 1)
    col = iota((wide, keys), 1)
    for c in range(ROWS // CHUNK):
        rows = pl.ds(c * CHUNK, CHUNK)
        qc = q[rows, :]
        qs = jnp.concatenate([qc[:, h * HEAD_DIM : (h + 1) * HEAD_DIM] for h in range(GROUP)], axis=0)
        kc = ck[pl.ds(c * keys, keys), :]
        vc = cv[pl.ds(c * keys, keys), :]
        scores = dot(qs, kc, ((1,), (1,))) * scale
        held = jnp.concatenate([lengths[c * CHUNK : (c + 1) * CHUNK, :]] * GROUP, axis=0)
        usable = (row_of == (col >> 5)) & ((col & 31) < held)
        scores = jnp.where(usable, scores, -jnp.inf)
        fresh_k = jnp.concatenate([nk[rows, :].astype(F32)] * GROUP, axis=0)
        fresh_v = jnp.concatenate([nv[rows, :].astype(F32)] * GROUP, axis=0)
        new_scores = jnp.sum(qs.astype(F32) * fresh_k, axis=1, keepdims=True) * scale
        highest = jnp.maximum(jnp.max(scores, axis=1, keepdims=True), new_scores)
        probs = jnp.exp(scores - highest)
        new_probs = jnp.exp(new_scores - highest)
        totals = jnp.sum(probs, axis=1, keepdims=True) + new_probs
        summed = dot(probs.astype(BF), vc) + new_probs.astype(BF).astype(F32) * fresh_v
        out = (summed / totals).astype(BF)
        for h in range(GROUP):
            att[rows, h * HEAD_DIM : (h + 1) * HEAD_DIM] = out[h * CHUNK : (h + 1) * CHUNK, :]
    everything = att[...]
    for g in range(PARTS):
        pick = picks[pl.ds(g * LINES, LINES), :]
        made[:, g * FEATS : (g + 1) * FEATS] = dot(pick, everything).astype(BF)
        leaving.append(leave(g, g * FEATS, FEATS))
    for copy in leaving:
        copy.wait()


def coefs_of(meta, g, first=0, count=ADP_DEV):
    shape = (128, count * RANK)
    line = iota(shape, 0)
    adapter = (iota(shape, 1) >> 6) + first
    spread = (line == adapter + g * 32) | (line == adapter + (g * 32 + ADP_DEV))
    return dot(meta, spread.astype(BF))


def join_parts(pieces):
    lane = iota((pieces[0].shape[0], 128), 1)
    first = jnp.where(lane < RANK, pieces[0], pieces[1])
    second = jnp.where(lane < RANK, pieces[2], 0.0)
    return jnp.concatenate([first, second], axis=1)


def lower_kernel(got, down, out, weights, sems):
    width = down.shape[1] // DOWN_STEPS
    copies = []
    for n in range(DOWN_STEPS):
        cols = pl.ds(n * width, width)
        copies.append(pltpu.make_async_copy(down.at[:, cols], weights.at[:, cols], sems.at[n]))
        copies[-1].start()
    meta = got[:, PARTS * FEATS :]
    coefs = [coefs_of(meta, g) for g in range(PARTS)]
    totals = [jnp.zeros((LINES, 128), F32)] * PARTS
    for n in range(DOWN_STEPS):
        copies[n].wait()
        block = weights[:, n * width : (n + 1) * width]
        for g in range(PARTS):
            lowered = dot(got[:, g * FEATS : (g + 1) * FEATS], block)
            lowered = lowered * coefs[g][:, n * width : (n + 1) * width]
            for p in range(width // 128):
                totals[g] = totals[g] + lowered[:, p * 128 : (p + 1) * 128]
    pieces = [total + pltpu.roll(total, RANK, 1) for total in totals]
    out[...] = join_parts(pieces).astype(BF)


def pick_kernel(ids, hub, after, picks, record):
    owner_of_line = iota((ROWS, LINES), 1) >> 3
    named = jnp.zeros((ROWS, LINES), jnp.bool_)
    lane = iota((ROWS, 128), 1) - RANK
    kept = jnp.zeros((ROWS, 128), F32)
    for j in range(TOPA):
        adapter = column(ids[j : j + 1, :].astype(F32)).astype(jnp.int32)
        owner = adapter >> 4
        named = named | (owner == owner_of_line)
        high, low = split_parts(column(hub[j : j + 1, :]))
        fields = (owner.astype(F32), (adapter & (ADP_DEV - 1)).astype(F32), high.astype(F32), low.astype(F32))
        for k, field in enumerate(fields):
            kept = jnp.where(lane == k * TOPA + j, field, kept)
    record[...] = kept.astype(BF)
    earlier = (iota((ROWS, ROWS), 1) < iota((ROWS, ROWS), 0)).astype(BF)
    place = dot(earlier, named.astype(BF)).astype(jnp.int32)
    place = jnp.where(named, place, -1)
    spot = iota((ROWS, LINES), 1) & (PART - 1)
    for g in range(PARTS):
        picks[pl.ds(g * ROWS, ROWS), :] = (place == spot + g * PART).astype(BF)


def home_kernel(got, picks, ahead, behind, out, far_low, far_high, sems):
    half = far_low.shape[0]
    copies = [
        pltpu.make_async_copy(ahead.at[pl.ds(0, half), :], far_low, sems.at[0]),
        pltpu.make_async_copy(behind.at[pl.ds(half, half), :], far_high, sems.at[1]),
    ]
    for copy in copies:
        copy.start()
    lane = iota((ROWS, 256), 1)
    total = jnp.zeros((ROWS, 256), F32)
    for g in range(PARTS):
        part = dot(picks[pl.ds(g * ROWS, ROWS), :], got[...])
        total = total + jnp.where((lane >> 6) == g, part, 0.0)
    folded = total[:, :128] + total[:, 128:]
    folded = folded + pltpu.roll(folded, RANK, 1)
    few = ROWS // 2
    lane = iota((few, 128), 1)
    out[...] = jnp.where(lane < RANK, folded[:few, :], folded[few:, :])
    for copy in copies:
        copy.wait()


def mix_kernel(own, ahead, behind, across, record, out):
    half = ROWS // 2
    total = (own[...] + ahead[...]) + (behind[...] + across[...])
    other = pltpu.roll(total, RANK, 1)
    mixed = jnp.concatenate([total, other], axis=0)
    lane = iota((ROWS, 128), 1)
    sent = jnp.where(lane < RANK, mixed, record[...].astype(F32)).astype(BF)
    for z in range(DEPTH):
        out[pl.ds(z * ROWS, ROWS), :] = sent


def raise_kernel(place, got, *refs):
    ups, (out, held, sems) = refs[: SIDES + 1], refs[SIDES + 1 :]
    half = held.shape[1] // 2
    copies = []
    for b in range(SIDES + 1):
        if b < SIDES - 1:
            target = held.at[b]
        else:
            target = held.at[SIDES - 1, pl.ds((b - SIDES + 1) * half, half), :]
        copies.append(pltpu.make_async_copy(ups[b], target, sems.at[b]))
        copies[-1].start()
    me = place[0, 0]
    y, z = me >> 3, me & (DEPTH - 1)
    rows = DEPTH * ROWS
    lane = iota((1, 128), 1)
    spot = lane & (RANK - 1)
    side = spot >> 4
    away = jnp.where(side == 3, 2, jnp.where(side == 2, 3, side))
    wanted = ((((y + away) & (SIDES - 1)) * DEPTH + z) * ADP_DEV + (spot & (ADP_DEV - 1))).astype(F32)
    record = got[...].astype(F32)
    lanes = iota((rows, 128), 1)
    coef = jnp.zeros((rows, 128), F32)
    for j in range(TOPA):
        owner, local, high, low = (
            record[:, RANK + k * TOPA + j : RANK + k * TOPA + j + 1] for k in range(4)
        )
        weight = jnp.where(lanes < RANK, high, low)
        coef = jnp.where(owner * ADP_DEV + local == wanted, weight, coef)
    coef = coef.astype(BF)
    mixed = jnp.where(lanes < RANK, record, pltpu.roll(record, RANK, 1))
    shape = (128, ADP_DEV * RANK)
    line = iota(shape, 0) & (RANK - 1)
    adapter = iota(shape, 1) >> 6
    total = jnp.zeros((rows, COLS), F32)
    for b in range(SIDES):
        coefs = dot(coef, (line == adapter + b * ADP_DEV).astype(BF))
        expanded = jnp.concatenate(
            [(coefs[:, p * 128 : (p + 1) * 128] * mixed).astype(BF) for p in range(ADP_DEV * RANK // 128)],
            axis=1,
        )
        copies[b].wait()
        if b == SIDES - 1:
            copies[SIDES].wait()
        total = total + dot(expanded, held[b])
    out[...] = total.astype(BF)


def final_kernel(got, frozen, out):
    total = frozen[...]
    for z in range(DEPTH):
        total = total + got[pl.ds(z * ROWS, ROWS), :].astype(F32)
    out[...] = total.astype(BF)


def home(got, picks, ahead, behind):
    half = shape_of(ahead.shape[0] // 2, ahead.shape[1])
    vmem, hbm = (pl.BlockSpec(memory_space=space) for space in (pltpu.VMEM, pltpu.HBM))
    return pl.pallas_call(
        home_kernel,
        out_shape=(shape_of(ROWS // 2, 128, dtype=F32), half, half),
        in_specs=[vmem, vmem, hbm, hbm],
        out_specs=(vmem, hbm, hbm),
        scratch_shapes=[pltpu.SemaphoreType.DMA((2,))],
        compiler_params=pltpu.CompilerParams(vmem_limit_bytes=24 * 1024 * 1024),
    )(got, picks, *[pltpu.with_memory_space_constraint(x, pltpu.HBM) for x in (ahead, behind)])


def lift(place, got, ups):
    return pl.pallas_call(
        raise_kernel,
        out_shape=shape_of(DEPTH * ROWS, COLS),
        in_specs=[pl.BlockSpec(memory_space=pltpu.SMEM), pl.BlockSpec(memory_space=pltpu.VMEM)]
        + [pl.BlockSpec(memory_space=pltpu.HBM)] * len(ups),
        scratch_shapes=[
            pltpu.VMEM((SIDES, *ups[0].shape), BF),
            pltpu.SemaphoreType.DMA((len(ups),)),
        ],
        compiler_params=pltpu.CompilerParams(vmem_limit_bytes=32 * 1024 * 1024),
    )(place, got, *[pltpu.with_memory_space_constraint(up, pltpu.HBM) for up in ups])


def attend(*args):
    return pl.pallas_call(
        attend_kernel,
        out_shape=(
            shape_of(ROWS, FEATS),
            shape_of(LINES, PARTS * FEATS + 128),
        ),
        in_specs=[pl.BlockSpec(memory_space=pltpu.HBM)] * len(args),
        out_specs=(
            pl.BlockSpec(memory_space=pltpu.VMEM),
            pl.BlockSpec(memory_space=pltpu.HBM),
        ),
        scratch_shapes=[pltpu.VMEM((PARTS * LINES, ROWS), BF)]
        + [pltpu.VMEM(x.shape, x.dtype) for x in args]
        + [
            pltpu.SemaphoreType.DMA((len(args),)),
            pltpu.VMEM((LINES, PARTS * FEATS + 128), BF),
            pltpu.SemaphoreType.DMA((PARTS + 1,)),
        ],
        compiler_params=pltpu.CompilerParams(vmem_limit_bytes=32 * 1024 * 1024),
    )(*[pltpu.with_memory_space_constraint(x, pltpu.HBM) for x in args])


def lower(got, down):
    return pl.pallas_call(
        lower_kernel,
        out_shape=shape_of(LINES, 256),
        in_specs=[pl.BlockSpec(memory_space=pltpu.VMEM), pl.BlockSpec(memory_space=pltpu.HBM)],
        scratch_shapes=[
            pltpu.VMEM(down.shape, down.dtype),
            pltpu.SemaphoreType.DMA((DOWN_STEPS,)),
        ],
        compiler_params=pltpu.CompilerParams(vmem_limit_bytes=24 * 1024 * 1024),
    )(got, pltpu.with_memory_space_constraint(down, pltpu.HBM))


def call(kernel, out_shape, *args):
    return pl.pallas_call(
        kernel,
        out_shape=out_shape,
        compiler_params=pltpu.CompilerParams(vmem_limit_bytes=24 * 1024 * 1024),
    )(*args)


def shape_of(*shape, dtype=BF):
    return jax.ShapeDtypeStruct(shape, dtype)


def swap(x, axis, groups=None):
    return lax.all_to_all(
        x, axis, split_axis=0, concat_axis=0, axis_index_groups=groups, tiled=True
    )


def beside(x, steps):
    pairs = [(i, (i // DEPTH - steps) % SIDES * DEPTH + i % DEPTH) for i in range(OWNERS)]
    return lax.ppermute(x, "adapter", pairs)


def turn(x, chips, cores):
    pairs = [
        (i, (i // CORES + chips) % CHIPS * CORES + (i + cores) % CORES) for i in range(TENSOR)
    ]
    return lax.ppermute(x, "tensor", pairs)


def frozen_sum(attended, out_weight):
    index = lax.axis_index("tensor")
    chip, core = index // CORES, index % CORES
    part = jnp.dot(attended, out_weight, preferred_element_type=F32)
    part = part.reshape(ROWS, CHIPS, CORES, COLS)
    kept = jnp.where(core == 0, part[:, :, 0], part[:, :, 1])
    sent = jnp.where(core == 0, part[:, :, 1], part[:, :, 0]).astype(BF)
    came = turn(sent, 0, 1)
    pair = (kept + came.astype(F32)).reshape(ROWS, CHIPS * COLS)
    rounded = pair.astype(BF)
    total = lax.dynamic_slice_in_dim(pair, chip * COLS, COLS, 1)
    for step in range(1, CHIPS):
        block = lax.dynamic_slice_in_dim(rounded, ((chip + step) % CHIPS) * COLS, COLS, 1)
        total = total + turn(block, step, 0).astype(F32)
    return total


def local(
    queries,
    cache_keys,
    cache_values,
    new_keys,
    new_values,
    cache_lengths,
    out_weight,
    adapter_down,
    adapter_up,
    adapter_ids,
    hub_weights,
):
    attended, payload = attend(
        queries,
        cache_keys.reshape(-1, HEAD_DIM),
        cache_values.reshape(-1, HEAD_DIM),
        new_keys,
        new_values,
        cache_lengths.reshape(1, ROWS),
        adapter_ids.T,
        hub_weights.T,
    )
    got = swap(payload, "adapter")
    frozen = frozen_sum(attended, out_weight)
    picks, record = call(
        pick_kernel,
        (shape_of(PARTS * ROWS, LINES), shape_of(ROWS, 128)),
        adapter_ids.T,
        hub_weights.T,
        attended,
    )
    later_up, attended = lax.optimization_barrier((adapter_up, attended))
    ahead, behind = beside(later_up, 1), beside(later_up, SIDES - 1)
    got, frozen, picks, record = lax.optimization_barrier((got, frozen, picks, record))
    lowered = lower(got, adapter_down)
    lowered = swap(lowered, "adapter")
    share, far_low, far_high = home(lowered, picks, ahead, behind)
    ups = (adapter_up, ahead, behind, beside(far_low, 1), beside(far_high, SIDES - 1))
    share = share + turn(share, 0, 1)
    shares = [turn(share, step, 0) for step in (1, CHIPS - 1, 2)]
    mixed = call(mix_kernel, shape_of(DEPTH * ROWS, 128), share, *shares, record)
    mixed = swap(mixed, "adapter", COLUMNS)
    place = lax.axis_index("adapter").reshape(1, 1)
    raised = swap(lift(place, mixed, ups), "adapter", COLUMNS)
    return call(final_kernel, shape_of(ROWS, COLS), raised, frozen)


def solution(mesh):
    return jax.shard_map(
        local,
        mesh=mesh,
        in_specs=(
            P("adapter", "tensor"),
            P("adapter", "tensor", None, None),
            P("adapter", "tensor", None, None),
            P("adapter", "tensor"),
            P("adapter", "tensor"),
            P("adapter"),
            P("tensor", None),
            P("tensor", "adapter"),
            P("adapter", "tensor"),
            P("adapter", None),
            P("adapter", None),
        ),
        out_specs=P("adapter", "tensor"),
        check_vma=False,
    )
```

```python
import functools
import math

import jax
import jax.numpy as jnp
from jax import lax
from jax.experimental import pallas as pl
from jax.experimental.pallas import tpu as pltpu
from jax.sharding import PartitionSpec as P

HEADS = 64
KV_HEADS = 8
GROUP = HEADS // KV_HEADS
HEAD_DIM = 128
RANK = 64
ADP_DEV = 16
TOPA = 4
CAP = 24
ROWS = 48
OWNERS = 32
PART = 8
PARTS = CAP // PART
LINES = OWNERS * PART
FEATS = GROUP * HEAD_DIM
COLS = 512
TENSOR = 8
CORES = 2
CHIPS = 4
DOWN_STEPS = 4
DEPTH = 8
SIDES = 4
COLUMNS = [[y * DEPTH + z for z in range(DEPTH)] for y in range(SIDES)]
CHUNK = 16
BF = jnp.bfloat16
F32 = jnp.float32


def iota(shape, dim):
    return lax.broadcasted_iota(jnp.int32, shape, dim)


def dot(a, b, contract=((1,), (0,))):
    return lax.dot_general(a, b, (contract, ((), ())), preferred_element_type=F32)


def column(line):
    diagonal = iota((ROWS, ROWS), 0) == iota((ROWS, ROWS), 1)
    return jnp.sum(jnp.where(diagonal, line, 0.0), axis=1, keepdims=True)


def split_parts(x):
    high = x.astype(BF)
    low = (x - high.astype(F32)).astype(BF)
    return high, low


def attend_kernel(
    q_hbm, ck_hbm, cv_hbm, nk_hbm, nv_hbm, lens_hbm, ids_hbm, hub_hbm,
    att, pay,
    picks, q, ck, cv, nk, nv, lens, ids, hub, sems, made, out_sems,
):
    def leave(g, start, width):
        cols = pl.ds(start, width)
        copy = pltpu.make_async_copy(made.at[:, cols], pay.at[:, cols], out_sems.at[g])
        copy.start()
        return copy

    copies = []
    sources = (ids_hbm, hub_hbm, lens_hbm, q_hbm, ck_hbm, nk_hbm, nv_hbm, cv_hbm)
    for n, (src, dst) in enumerate(zip(sources, (ids, hub, lens, q, ck, nk, nv, cv))):
        copies.append(pltpu.make_async_copy(src, dst, sems.at[n]))
        copies[-1].start()

    copies[0].wait()
    copies[1].wait()
    shape = (LINES, ROWS)
    owner_of_line = iota(shape, 0) >> 3
    hits = [(ids[j : j + 1, :] >> 4) == owner_of_line for j in range(TOPA)]
    named = (hits[0] | hits[1]) | (hits[2] | hits[3])
    earlier = (iota((ROWS, ROWS), 0) < iota((ROWS, ROWS), 1)).astype(BF)
    place = dot(named.astype(BF), earlier).astype(jnp.int32)
    place = jnp.where(named, place, -1)
    spot = iota(shape, 0) & (PART - 1)
    line = iota((128, ROWS), 0)
    spreads = []
    for j in range(TOPA):
        within = ids[j : j + 1, :] & (ADP_DEV - 1)
        high, low = split_parts(hub[j : j + 1, :])
        spread = jnp.where(line == within, high.astype(F32), 0.0)
        spread = jnp.where(line == within + ADP_DEV, low.astype(F32), spread)
        spreads.append(spread.astype(BF))
    meta = jnp.zeros((LINES, 128), F32)
    for g in range(PARTS):
        pick = place == spot + g * PART
        picks[pl.ds(g * LINES, LINES), :] = pick.astype(BF)
        coefs = jnp.zeros((LINES, 128), F32)
        for j in range(TOPA):
            coefs = coefs + dot((pick & hits[j]).astype(BF), spreads[j], ((1,), (1,)))
        meta = meta + (pltpu.roll(coefs, g * 2 * ADP_DEV, 1) if g else coefs)
    made[:, PARTS * FEATS :] = meta.astype(BF)
    leaving = [leave(PARTS, PARTS * FEATS, 128)]

    for copy in copies[2:]:
        copy.wait()
    lengths = column(lens[...].astype(F32)).astype(jnp.int32)
    scale = 1.0 / math.sqrt(HEAD_DIM)
    keys = CHUNK * 32
    wide = CHUNK * GROUP
    row_of = iota((wide, keys), 0) & (CHUNK - 1)
    col = iota((wide, keys), 1)
    for c in range(ROWS // CHUNK):
        rows = pl.ds(c * CHUNK, CHUNK)
        qc = q[rows, :]
        qs = jnp.concatenate([qc[:, h * HEAD_DIM : (h + 1) * HEAD_DIM] for h in range(GROUP)], axis=0)
        kc = ck[pl.ds(c * keys, keys), :]
        vc = cv[pl.ds(c * keys, keys), :]
        scores = dot(qs, kc, ((1,), (1,))) * scale
        held = jnp.concatenate([lengths[c * CHUNK : (c + 1) * CHUNK, :]] * GROUP, axis=0)
        usable = (row_of == (col >> 5)) & ((col & 31) < held)
        scores = jnp.where(usable, scores, -jnp.inf)
        fresh_k = jnp.concatenate([nk[rows, :].astype(F32)] * GROUP, axis=0)
        fresh_v = jnp.concatenate([nv[rows, :].astype(F32)] * GROUP, axis=0)
        new_scores = jnp.sum(qs.astype(F32) * fresh_k, axis=1, keepdims=True) * scale
        highest = jnp.maximum(jnp.max(scores, axis=1, keepdims=True), new_scores)
        probs = jnp.exp(scores - highest)
        new_probs = jnp.exp(new_scores - highest)
        totals = jnp.sum(probs, axis=1, keepdims=True) + new_probs
        summed = dot(probs.astype(BF), vc) + new_probs.astype(BF).astype(F32) * fresh_v
        out = (summed / totals).astype(BF)
        for h in range(GROUP):
            att[rows, h * HEAD_DIM : (h + 1) * HEAD_DIM] = out[h * CHUNK : (h + 1) * CHUNK, :]
    everything = att[...]
    for g in range(PARTS):
        pick = picks[pl.ds(g * LINES, LINES), :]
        made[:, g * FEATS : (g + 1) * FEATS] = dot(pick, everything).astype(BF)
        leaving.append(leave(g, g * FEATS, FEATS))
    for copy in leaving:
        copy.wait()


def coefs_of(meta, g, first=0, count=ADP_DEV):
    shape = (128, count * RANK)
    line = iota(shape, 0)
    adapter = (iota(shape, 1) >> 6) + first
    spread = (line == adapter + g * 32) | (line == adapter + (g * 32 + ADP_DEV))
    return dot(meta, spread.astype(BF))


def join_parts(pieces):
    lane = iota((pieces[0].shape[0], 128), 1)
    first = jnp.where(lane < RANK, pieces[0], pieces[1])
    second = jnp.where(lane < RANK, pieces[2], 0.0)
    return jnp.concatenate([first, second], axis=1)


def lower_kernel(got, down, out, weights, sems):
    width = down.shape[1] // DOWN_STEPS
    copies = []
    for n in range(DOWN_STEPS):
        cols = pl.ds(n * width, width)
        copies.append(pltpu.make_async_copy(down.at[:, cols], weights.at[:, cols], sems.at[n]))
        copies[-1].start()
    meta = got[:, PARTS * FEATS :]
    coefs = [coefs_of(meta, g) for g in range(PARTS)]
    totals = [jnp.zeros((LINES, 128), F32)] * PARTS
    for n in range(DOWN_STEPS):
        copies[n].wait()
        block = weights[:, n * width : (n + 1) * width]
        for g in range(PARTS):
            lowered = dot(got[:, g * FEATS : (g + 1) * FEATS], block)
            lowered = lowered * coefs[g][:, n * width : (n + 1) * width]
            for p in range(width // 128):
                totals[g] = totals[g] + lowered[:, p * 128 : (p + 1) * 128]
    pieces = [total + pltpu.roll(total, RANK, 1) for total in totals]
    out[...] = join_parts(pieces).astype(BF)


def pick_kernel(ids, hub, after, picks, record):
    owner_of_line = iota((ROWS, LINES), 1) >> 3
    named = jnp.zeros((ROWS, LINES), jnp.bool_)
    lane = iota((ROWS, 128), 1) - RANK
    kept = jnp.zeros((ROWS, 128), F32)
    for j in range(TOPA):
        adapter = column(ids[j : j + 1, :].astype(F32)).astype(jnp.int32)
        owner = adapter >> 4
        named = named | (owner == owner_of_line)
        high, low = split_parts(column(hub[j : j + 1, :]))
        fields = (owner.astype(F32), (adapter & (ADP_DEV - 1)).astype(F32), high.astype(F32), low.astype(F32))
        for k, field in enumerate(fields):
            kept = jnp.where(lane == k * TOPA + j, field, kept)
    record[...] = kept.astype(BF)
    earlier = (iota((ROWS, ROWS), 1) < iota((ROWS, ROWS), 0)).astype(BF)
    place = dot(earlier, named.astype(BF)).astype(jnp.int32)
    place = jnp.where(named, place, -1)
    spot = iota((ROWS, LINES), 1) & (PART - 1)
    for g in range(PARTS):
        picks[pl.ds(g * ROWS, ROWS), :] = (place == spot + g * PART).astype(BF)


def split_kernel(ahead, behind, far_low, far_high, sems):
    half = far_low.shape[0]
    copies = [
        pltpu.make_async_copy(ahead.at[pl.ds(0, half), :], far_low, sems.at[0]),
        pltpu.make_async_copy(behind.at[pl.ds(half, half), :], far_high, sems.at[1]),
    ]
    for copy in copies:
        copy.start()
    for copy in copies:
        copy.wait()


def home_kernel(got, picks, out):
    lane = iota((ROWS, 256), 1)
    total = jnp.zeros((ROWS, 256), F32)
    for g in range(PARTS):
        part = dot(picks[pl.ds(g * ROWS, ROWS), :], got[...])
        total = total + jnp.where((lane >> 6) == g, part, 0.0)
    folded = total[:, :128] + total[:, 128:]
    folded = folded + pltpu.roll(folded, RANK, 1)
    half = ROWS // 2
    lane = iota((half, 128), 1)
    out[...] = jnp.where(lane < RANK, folded[:half, :], folded[half:, :])


def mix_kernel(own, ahead, behind, across, record, out):
    half = ROWS // 2
    total = (own[...] + ahead[...]) + (behind[...] + across[...])
    other = pltpu.roll(total, RANK, 1)
    mixed = jnp.concatenate([total, other], axis=0)
    lane = iota((ROWS, 128), 1)
    sent = jnp.where(lane < RANK, mixed, record[...].astype(F32)).astype(BF)
    for z in range(DEPTH):
        out[pl.ds(z * ROWS, ROWS), :] = sent


def raise_kernel(place, got, *refs):
    ups, (out, held, sems) = refs[: SIDES + 1], refs[SIDES + 1 :]
    half = held.shape[1] // 2
    copies = []
    for b in range(SIDES + 1):
        if b < SIDES - 1:
            target = held.at[b]
        else:
            target = held.at[SIDES - 1, pl.ds((b - SIDES + 1) * half, half), :]
        copies.append(pltpu.make_async_copy(ups[b], target, sems.at[b]))
        copies[-1].start()
    me = place[0, 0]
    y, z = me >> 3, me & (DEPTH - 1)
    rows = DEPTH * ROWS
    lane = iota((1, 128), 1)
    spot = lane & (RANK - 1)
    side = spot >> 4
    away = jnp.where(side == 3, 2, jnp.where(side == 2, 3, side))
    wanted = ((((y + away) & (SIDES - 1)) * DEPTH + z) * ADP_DEV + (spot & (ADP_DEV - 1))).astype(F32)
    record = got[...].astype(F32)
    lanes = iota((rows, 128), 1)
    coef = jnp.zeros((rows, 128), F32)
    for j in range(TOPA):
        owner, local, high, low = (
            record[:, RANK + k * TOPA + j : RANK + k * TOPA + j + 1] for k in range(4)
        )
        weight = jnp.where(lanes < RANK, high, low)
        coef = jnp.where(owner * ADP_DEV + local == wanted, weight, coef)
    coef = coef.astype(BF)
    mixed = jnp.where(lanes < RANK, record, pltpu.roll(record, RANK, 1))
    shape = (128, ADP_DEV * RANK)
    line = iota(shape, 0) & (RANK - 1)
    adapter = iota(shape, 1) >> 6
    total = jnp.zeros((rows, COLS), F32)
    for b in range(SIDES):
        coefs = dot(coef, (line == adapter + b * ADP_DEV).astype(BF))
        expanded = jnp.concatenate(
            [(coefs[:, p * 128 : (p + 1) * 128] * mixed).astype(BF) for p in range(ADP_DEV * RANK // 128)],
            axis=1,
        )
        copies[b].wait()
        if b == SIDES - 1:
            copies[SIDES].wait()
        total = total + dot(expanded, held[b])
    out[...] = total.astype(BF)


def final_kernel(got, frozen, out):
    total = frozen[...]
    for z in range(DEPTH):
        total = total + got[pl.ds(z * ROWS, ROWS), :].astype(F32)
    out[...] = total.astype(BF)


def split(ahead, behind):
    half = shape_of(ahead.shape[0] // 2, ahead.shape[1])
    hbm = pl.BlockSpec(memory_space=pltpu.HBM)
    return pl.pallas_call(
        split_kernel,
        out_shape=(half, half),
        in_specs=[hbm, hbm],
        out_specs=(hbm, hbm),
        scratch_shapes=[pltpu.SemaphoreType.DMA((2,))],
        compiler_params=pltpu.CompilerParams(vmem_limit_bytes=24 * 1024 * 1024),
    )(*[pltpu.with_memory_space_constraint(x, pltpu.HBM) for x in (ahead, behind)])


def lift(place, got, ups):
    return pl.pallas_call(
        raise_kernel,
        out_shape=shape_of(DEPTH * ROWS, COLS),
        in_specs=[pl.BlockSpec(memory_space=pltpu.SMEM), pl.BlockSpec(memory_space=pltpu.VMEM)]
        + [pl.BlockSpec(memory_space=pltpu.HBM)] * 3
        + [pl.BlockSpec(memory_space=pl.ANY)] * 2,
        scratch_shapes=[
            pltpu.VMEM((SIDES, *ups[0].shape), BF),
            pltpu.SemaphoreType.DMA((len(ups),)),
        ],
        compiler_params=pltpu.CompilerParams(vmem_limit_bytes=32 * 1024 * 1024),
    )(place, got, *[pltpu.with_memory_space_constraint(up, pltpu.HBM) for up in ups[:3]], *ups[3:])


def attend(*args):
    return pl.pallas_call(
        attend_kernel,
        out_shape=(
            shape_of(ROWS, FEATS),
            shape_of(LINES, PARTS * FEATS + 128),
        ),
        in_specs=[pl.BlockSpec(memory_space=pltpu.HBM)] * len(args),
        out_specs=(
            pl.BlockSpec(memory_space=pltpu.VMEM),
            pl.BlockSpec(memory_space=pltpu.HBM),
        ),
        scratch_shapes=[pltpu.VMEM((PARTS * LINES, ROWS), BF)]
        + [pltpu.VMEM(x.shape, x.dtype) for x in args]
        + [
            pltpu.SemaphoreType.DMA((len(args),)),
            pltpu.VMEM((LINES, PARTS * FEATS + 128), BF),
            pltpu.SemaphoreType.DMA((PARTS + 1,)),
        ],
        compiler_params=pltpu.CompilerParams(vmem_limit_bytes=32 * 1024 * 1024),
    )(*[pltpu.with_memory_space_constraint(x, pltpu.HBM) for x in args])


def lower(got, down):
    return pl.pallas_call(
        lower_kernel,
        out_shape=shape_of(LINES, 256),
        in_specs=[pl.BlockSpec(memory_space=pltpu.VMEM), pl.BlockSpec(memory_space=pltpu.HBM)],
        scratch_shapes=[
            pltpu.VMEM(down.shape, down.dtype),
            pltpu.SemaphoreType.DMA((DOWN_STEPS,)),
        ],
        compiler_params=pltpu.CompilerParams(vmem_limit_bytes=24 * 1024 * 1024),
    )(got, pltpu.with_memory_space_constraint(down, pltpu.HBM))


def call(kernel, out_shape, *args):
    return pl.pallas_call(
        kernel,
        out_shape=out_shape,
        compiler_params=pltpu.CompilerParams(vmem_limit_bytes=24 * 1024 * 1024),
    )(*args)


def shape_of(*shape, dtype=BF):
    return jax.ShapeDtypeStruct(shape, dtype)


def swap(x, axis, groups=None):
    return lax.all_to_all(
        x, axis, split_axis=0, concat_axis=0, axis_index_groups=groups, tiled=True
    )


def beside(x, steps):
    pairs = [(i, (i // DEPTH - steps) % SIDES * DEPTH + i % DEPTH) for i in range(OWNERS)]
    return lax.ppermute(x, "adapter", pairs)


def turn(x, chips, cores):
    pairs = [
        (i, (i // CORES + chips) % CHIPS * CORES + (i + cores) % CORES) for i in range(TENSOR)
    ]
    return lax.ppermute(x, "tensor", pairs)


def frozen_sum(attended, out_weight):
    index = lax.axis_index("tensor")
    chip, core = index // CORES, index % CORES
    part = jnp.dot(attended, out_weight, preferred_element_type=F32)
    part = part.reshape(ROWS, CHIPS, CORES, COLS)
    kept = jnp.where(core == 0, part[:, :, 0], part[:, :, 1])
    sent = jnp.where(core == 0, part[:, :, 1], part[:, :, 0]).astype(BF)
    came = turn(sent, 0, 1)
    pair = (kept + came.astype(F32)).reshape(ROWS, CHIPS * COLS)
    rounded = pair.astype(BF)
    total = lax.dynamic_slice_in_dim(pair, chip * COLS, COLS, 1)
    for step in range(1, CHIPS):
        block = lax.dynamic_slice_in_dim(rounded, ((chip + step) % CHIPS) * COLS, COLS, 1)
        total = total + turn(block, step, 0).astype(F32)
    return total


def local(
    queries,
    cache_keys,
    cache_values,
    new_keys,
    new_values,
    cache_lengths,
    out_weight,
    adapter_down,
    adapter_up,
    adapter_ids,
    hub_weights,
):
    attended, payload = attend(
        queries,
        cache_keys.reshape(-1, HEAD_DIM),
        cache_values.reshape(-1, HEAD_DIM),
        new_keys,
        new_values,
        cache_lengths.reshape(1, ROWS),
        adapter_ids.T,
        hub_weights.T,
    )
    got = swap(payload, "adapter")
    frozen = frozen_sum(attended, out_weight)
    picks, record = call(
        pick_kernel,
        (shape_of(PARTS * ROWS, LINES), shape_of(ROWS, 128)),
        adapter_ids.T,
        hub_weights.T,
        attended,
    )
    later_up, attended = lax.optimization_barrier((adapter_up, attended))
    ahead, behind = beside(later_up, 1), beside(later_up, SIDES - 1)
    got, frozen, picks, record = lax.optimization_barrier((got, frozen, picks, record))
    lowered = lower(got, adapter_down)
    lowered = swap(lowered, "adapter")
    far_low, far_high = split(ahead, behind)
    lowered, far_low, far_high = lax.optimization_barrier((lowered, far_low, far_high))
    share = call(home_kernel, shape_of(ROWS // 2, 128, dtype=F32), lowered, picks)
    share = share + turn(share, 0, 1)
    share, far_low, far_high = lax.optimization_barrier((share, far_low, far_high))
    shares = [turn(share, step, 0) for step in (1, CHIPS - 1, 2)]
    ups = (adapter_up, ahead, behind, beside(far_low, 1), beside(far_high, SIDES - 1))
    mixed = call(mix_kernel, shape_of(DEPTH * ROWS, 128), share, *shares, record)
    mixed = swap(mixed, "adapter", COLUMNS)
    place = lax.axis_index("adapter").reshape(1, 1)
    raised = swap(lift(place, mixed, ups), "adapter", COLUMNS)
    return call(final_kernel, shape_of(ROWS, COLS), raised, frozen)


def solution(mesh):
    return jax.shard_map(
        local,
        mesh=mesh,
        in_specs=(
            P("adapter", "tensor"),
            P("adapter", "tensor", None, None),
            P("adapter", "tensor", None, None),
            P("adapter", "tensor"),
            P("adapter", "tensor"),
            P("adapter"),
            P("tensor", None),
            P("tensor", "adapter"),
            P("adapter", "tensor"),
            P("adapter", None),
            P("adapter", None),
        ),
        out_specs=P("adapter", "tensor"),
        check_vma=False,
    )
```

```python
import functools
import math

import jax
import jax.numpy as jnp
from jax import lax
from jax.experimental import pallas as pl
from jax.experimental.pallas import tpu as pltpu
from jax.sharding import PartitionSpec as P

HEADS = 64
KV_HEADS = 8
GROUP = HEADS // KV_HEADS
HEAD_DIM = 128
RANK = 64
ADP_DEV = 16
TOPA = 4
CAP = 24
ROWS = 48
OWNERS = 32
PART = 8
PARTS = CAP // PART
LINES = OWNERS * PART
FEATS = GROUP * HEAD_DIM
COLS = 512
TENSOR = 8
CORES = 2
CHIPS = 4
DOWN_STEPS = 2
DEPTH = 8
SIDES = 4
COLUMNS = [[y * DEPTH + z for z in range(DEPTH)] for y in range(SIDES)]
CHUNK = 16
BF = jnp.bfloat16
F32 = jnp.float32


def iota(shape, dim):
    return lax.broadcasted_iota(jnp.int32, shape, dim)


def dot(a, b, contract=((1,), (0,))):
    return lax.dot_general(a, b, (contract, ((), ())), preferred_element_type=F32)


def column(line):
    diagonal = iota((ROWS, ROWS), 0) == iota((ROWS, ROWS), 1)
    return jnp.sum(jnp.where(diagonal, line, 0.0), axis=1, keepdims=True)


def split_parts(x):
    high = x.astype(BF)
    low = (x - high.astype(F32)).astype(BF)
    return high, low


def attend_kernel(
    q_hbm, ck_hbm, cv_hbm, nk_hbm, nv_hbm, lens_hbm, ids_hbm, hub_hbm,
    att, pay,
    picks, q, ck, cv, nk, nv, lens, ids, hub, sems, made, out_sems,
):
    def leave(g, start, width):
        cols = pl.ds(start, width)
        copy = pltpu.make_async_copy(made.at[:, cols], pay.at[:, cols], out_sems.at[g])
        copy.start()
        return copy

    copies = []
    sources = (ids_hbm, hub_hbm, lens_hbm, q_hbm, ck_hbm, nk_hbm, nv_hbm, cv_hbm)
    for n, (src, dst) in enumerate(zip(sources, (ids, hub, lens, q, ck, nk, nv, cv))):
        copies.append(pltpu.make_async_copy(src, dst, sems.at[n]))
        copies[-1].start()

    copies[0].wait()
    copies[1].wait()
    shape = (LINES, ROWS)
    owner_of_line = iota(shape, 0) >> 3
    hits = [(ids[j : j + 1, :] >> 4) == owner_of_line for j in range(TOPA)]
    named = (hits[0] | hits[1]) | (hits[2] | hits[3])
    earlier = (iota((ROWS, ROWS), 0) < iota((ROWS, ROWS), 1)).astype(BF)
    place = dot(named.astype(BF), earlier).astype(jnp.int32)
    place = jnp.where(named, place, -1)
    spot = iota(shape, 0) & (PART - 1)
    line = iota((128, ROWS), 0)
    spreads = []
    for j in range(TOPA):
        within = ids[j : j + 1, :] & (ADP_DEV - 1)
        high, low = split_parts(hub[j : j + 1, :])
        spread = jnp.where(line == within, high.astype(F32), 0.0)
        spread = jnp.where(line == within + ADP_DEV, low.astype(F32), spread)
        spreads.append(spread.astype(BF))
    meta = jnp.zeros((LINES, 128), F32)
    for g in range(PARTS):
        pick = place == spot + g * PART
        picks[pl.ds(g * LINES, LINES), :] = pick.astype(BF)
        coefs = jnp.zeros((LINES, 128), F32)
        for j in range(TOPA):
            coefs = coefs + dot((pick & hits[j]).astype(BF), spreads[j], ((1,), (1,)))
        meta = meta + (pltpu.roll(coefs, g * 2 * ADP_DEV, 1) if g else coefs)
    made[:, PARTS * FEATS :] = meta.astype(BF)
    leaving = [leave(PARTS, PARTS * FEATS, 128)]

    for copy in copies[2:]:
        copy.wait()
    lengths = column(lens[...].astype(F32)).astype(jnp.int32)
    scale = 1.0 / math.sqrt(HEAD_DIM)
    keys = CHUNK * 32
    wide = CHUNK * GROUP
    row_of = iota((wide, keys), 0) & (CHUNK - 1)
    col = iota((wide, keys), 1)
    for c in range(ROWS // CHUNK):
        rows = pl.ds(c * CHUNK, CHUNK)
        qc = q[rows, :]
        qs = jnp.concatenate([qc[:, h * HEAD_DIM : (h + 1) * HEAD_DIM] for h in range(GROUP)], axis=0)
        kc = ck[pl.ds(c * keys, keys), :]
        vc = cv[pl.ds(c * keys, keys), :]
        scores = dot(qs, kc, ((1,), (1,))) * scale
        held = jnp.concatenate([lengths[c * CHUNK : (c + 1) * CHUNK, :]] * GROUP, axis=0)
        usable = (row_of == (col >> 5)) & ((col & 31) < held)
        scores = jnp.where(usable, scores, -jnp.inf)
        fresh_k = jnp.concatenate([nk[rows, :].astype(F32)] * GROUP, axis=0)
        fresh_v = jnp.concatenate([nv[rows, :].astype(F32)] * GROUP, axis=0)
        new_scores = jnp.sum(qs.astype(F32) * fresh_k, axis=1, keepdims=True) * scale
        highest = jnp.maximum(jnp.max(scores, axis=1, keepdims=True), new_scores)
        probs = jnp.exp(scores - highest)
        new_probs = jnp.exp(new_scores - highest)
        totals = jnp.sum(probs, axis=1, keepdims=True) + new_probs
        summed = dot(probs.astype(BF), vc) + new_probs.astype(BF).astype(F32) * fresh_v
        out = (summed / totals).astype(BF)
        for h in range(GROUP):
            att[rows, h * HEAD_DIM : (h + 1) * HEAD_DIM] = out[h * CHUNK : (h + 1) * CHUNK, :]
    everything = att[...]
    for g in range(PARTS):
        pick = picks[pl.ds(g * LINES, LINES), :]
        made[:, g * FEATS : (g + 1) * FEATS] = dot(pick, everything).astype(BF)
        leaving.append(leave(g, g * FEATS, FEATS))
    for copy in leaving:
        copy.wait()


def coefs_of(meta, g, first=0, count=ADP_DEV):
    shape = (128, count * RANK)
    line = iota(shape, 0)
    adapter = (iota(shape, 1) >> 6) + first
    spread = (line == adapter + g * 32) | (line == adapter + (g * 32 + ADP_DEV))
    return dot(meta, spread.astype(BF))


def join_parts(pieces):
    lane = iota((pieces[0].shape[0], 128), 1)
    first = jnp.where(lane < RANK, pieces[0], pieces[1])
    second = jnp.where(lane < RANK, pieces[2], 0.0)
    return jnp.concatenate([first, second], axis=1)


def lower_kernel(got, down, out, weights, sems):
    width = down.shape[1] // DOWN_STEPS
    copies = []
    for n in range(DOWN_STEPS):
        cols = pl.ds(n * width, width)
        copies.append(pltpu.make_async_copy(down.at[:, cols], weights.at[:, cols], sems.at[n]))
        copies[-1].start()
    meta = got[:, PARTS * FEATS :]
    coefs = [coefs_of(meta, g) for g in range(PARTS)]
    totals = [jnp.zeros((LINES, 128), F32)] * PARTS
    for n in range(DOWN_STEPS):
        copies[n].wait()
        block = weights[:, n * width : (n + 1) * width]
        for g in range(PARTS):
            lowered = dot(got[:, g * FEATS : (g + 1) * FEATS], block)
            lowered = lowered * coefs[g][:, n * width : (n + 1) * width]
            for p in range(width // 128):
                totals[g] = totals[g] + lowered[:, p * 128 : (p + 1) * 128]
    pieces = [total + pltpu.roll(total, RANK, 1) for total in totals]
    out[...] = join_parts(pieces).astype(BF)


def pick_kernel(ids, hub, after, picks, record):
    owner_of_line = iota((ROWS, LINES), 1) >> 3
    named = jnp.zeros((ROWS, LINES), jnp.bool_)
    lane = iota((ROWS, 128), 1) - RANK
    kept = jnp.zeros((ROWS, 128), F32)
    for j in range(TOPA):
        adapter = column(ids[j : j + 1, :].astype(F32)).astype(jnp.int32)
        owner = adapter >> 4
        named = named | (owner == owner_of_line)
        high, low = split_parts(column(hub[j : j + 1, :]))
        fields = (owner.astype(F32), (adapter & (ADP_DEV - 1)).astype(F32), high.astype(F32), low.astype(F32))
        for k, field in enumerate(fields):
            kept = jnp.where(lane == k * TOPA + j, field, kept)
    record[...] = kept.astype(BF)
    earlier = (iota((ROWS, ROWS), 1) < iota((ROWS, ROWS), 0)).astype(BF)
    place = dot(earlier, named.astype(BF)).astype(jnp.int32)
    place = jnp.where(named, place, -1)
    spot = iota((ROWS, LINES), 1) & (PART - 1)
    for g in range(PARTS):
        picks[pl.ds(g * ROWS, ROWS), :] = (place == spot + g * PART).astype(BF)


def split_kernel(ahead, behind, far_low, far_high, sems):
    half = far_low.shape[0]
    copies = [
        pltpu.make_async_copy(ahead.at[pl.ds(0, half), :], far_low, sems.at[0]),
        pltpu.make_async_copy(behind.at[pl.ds(half, half), :], far_high, sems.at[1]),
    ]
    for copy in copies:
        copy.start()
    for copy in copies:
        copy.wait()


def home_kernel(got, picks, out):
    lane = iota((ROWS, 256), 1)
    total = jnp.zeros((ROWS, 256), F32)
    for g in range(PARTS):
        part = dot(picks[pl.ds(g * ROWS, ROWS), :], got[...])
        total = total + jnp.where((lane >> 6) == g, part, 0.0)
    folded = total[:, :128] + total[:, 128:]
    folded = folded + pltpu.roll(folded, RANK, 1)
    half = ROWS // 2
    lane = iota((half, 128), 1)
    out[...] = jnp.where(lane < RANK, folded[:half, :], folded[half:, :])


def mix_kernel(own, ahead, behind, across, record, out):
    half = ROWS // 2
    total = (own[...] + ahead[...]) + (behind[...] + across[...])
    other = pltpu.roll(total, RANK, 1)
    mixed = jnp.concatenate([total, other], axis=0)
    lane = iota((ROWS, 128), 1)
    sent = jnp.where(lane < RANK, mixed, record[...].astype(F32)).astype(BF)
    for z in range(DEPTH):
        out[pl.ds(z * ROWS, ROWS), :] = sent


def raise_kernel(place, got, *refs):
    ups, (out, held, sems) = refs[: SIDES + 1], refs[SIDES + 1 :]
    half = held.shape[1] // 2
    copies = []
    for b in range(SIDES + 1):
        if b < SIDES - 1:
            target = held.at[b]
        else:
            target = held.at[SIDES - 1, pl.ds((b - SIDES + 1) * half, half), :]
        copies.append(pltpu.make_async_copy(ups[b], target, sems.at[b]))
        copies[-1].start()
    me = place[0, 0]
    y, z = me >> 3, me & (DEPTH - 1)
    rows = DEPTH * ROWS
    lane = iota((1, 128), 1)
    spot = lane & (RANK - 1)
    side = spot >> 4
    away = jnp.where(side == 3, 2, jnp.where(side == 2, 3, side))
    wanted = ((((y + away) & (SIDES - 1)) * DEPTH + z) * ADP_DEV + (spot & (ADP_DEV - 1))).astype(F32)
    record = got[...].astype(F32)
    lanes = iota((rows, 128), 1)
    coef = jnp.zeros((rows, 128), F32)
    for j in range(TOPA):
        owner, local, high, low = (
            record[:, RANK + k * TOPA + j : RANK + k * TOPA + j + 1] for k in range(4)
        )
        weight = jnp.where(lanes < RANK, high, low)
        coef = jnp.where(owner * ADP_DEV + local == wanted, weight, coef)
    coef = coef.astype(BF)
    mixed = jnp.where(lanes < RANK, record, pltpu.roll(record, RANK, 1))
    shape = (128, ADP_DEV * RANK)
    line = iota(shape, 0) & (RANK - 1)
    adapter = iota(shape, 1) >> 6
    blocks = []
    for b in range(SIDES):
        coefs = dot(coef, (line == adapter + b * ADP_DEV).astype(BF))
        for p in range(ADP_DEV * RANK // 128):
            blocks.append((coefs[:, p * 128 : (p + 1) * 128] * mixed).astype(BF))
    for copy in copies:
        copy.wait()
    total = dot(jnp.concatenate(blocks, axis=1), held[...].reshape(SIDES * ADP_DEV * RANK, COLS))
    out[...] = total.astype(BF)


def final_kernel(got, frozen, out):
    total = frozen[...]
    for z in range(DEPTH):
        total = total + got[pl.ds(z * ROWS, ROWS), :].astype(F32)
    out[...] = total.astype(BF)


def split(ahead, behind):
    half = shape_of(ahead.shape[0] // 2, ahead.shape[1])
    hbm = pl.BlockSpec(memory_space=pltpu.HBM)
    return pl.pallas_call(
        split_kernel,
        out_shape=(half, half),
        in_specs=[hbm, hbm],
        out_specs=(hbm, hbm),
        scratch_shapes=[pltpu.SemaphoreType.DMA((2,))],
        compiler_params=pltpu.CompilerParams(vmem_limit_bytes=24 * 1024 * 1024),
    )(*[pltpu.with_memory_space_constraint(x, pltpu.HBM) for x in (ahead, behind)])


def lift(place, got, ups):
    return pl.pallas_call(
        raise_kernel,
        out_shape=shape_of(DEPTH * ROWS, COLS),
        in_specs=[pl.BlockSpec(memory_space=pltpu.SMEM), pl.BlockSpec(memory_space=pltpu.VMEM)]
        + [pl.BlockSpec(memory_space=pltpu.HBM)] * 3
        + [pl.BlockSpec(memory_space=pl.ANY)] * 2,
        scratch_shapes=[
            pltpu.VMEM((SIDES, *ups[0].shape), BF),
            pltpu.SemaphoreType.DMA((len(ups),)),
        ],
        compiler_params=pltpu.CompilerParams(vmem_limit_bytes=32 * 1024 * 1024),
    )(place, got, *[pltpu.with_memory_space_constraint(up, pltpu.HBM) for up in ups[:3]], *ups[3:])


def attend(*args):
    return pl.pallas_call(
        attend_kernel,
        out_shape=(
            shape_of(ROWS, FEATS),
            shape_of(LINES, PARTS * FEATS + 128),
        ),
        in_specs=[pl.BlockSpec(memory_space=pltpu.HBM)] * len(args),
        out_specs=(
            pl.BlockSpec(memory_space=pltpu.VMEM),
            pl.BlockSpec(memory_space=pltpu.HBM),
        ),
        scratch_shapes=[pltpu.VMEM((PARTS * LINES, ROWS), BF)]
        + [pltpu.VMEM(x.shape, x.dtype) for x in args]
        + [
            pltpu.SemaphoreType.DMA((len(args),)),
            pltpu.VMEM((LINES, PARTS * FEATS + 128), BF),
            pltpu.SemaphoreType.DMA((PARTS + 1,)),
        ],
        compiler_params=pltpu.CompilerParams(vmem_limit_bytes=32 * 1024 * 1024),
    )(*[pltpu.with_memory_space_constraint(x, pltpu.HBM) for x in args])


def lower(got, down):
    return pl.pallas_call(
        lower_kernel,
        out_shape=shape_of(LINES, 256),
        in_specs=[pl.BlockSpec(memory_space=pltpu.VMEM), pl.BlockSpec(memory_space=pltpu.HBM)],
        scratch_shapes=[
            pltpu.VMEM(down.shape, down.dtype),
            pltpu.SemaphoreType.DMA((DOWN_STEPS,)),
        ],
        compiler_params=pltpu.CompilerParams(vmem_limit_bytes=24 * 1024 * 1024),
    )(got, pltpu.with_memory_space_constraint(down, pltpu.HBM))


def call(kernel, out_shape, *args):
    return pl.pallas_call(
        kernel,
        out_shape=out_shape,
        compiler_params=pltpu.CompilerParams(vmem_limit_bytes=24 * 1024 * 1024),
    )(*args)


def shape_of(*shape, dtype=BF):
    return jax.ShapeDtypeStruct(shape, dtype)


def swap(x, axis, groups=None):
    return lax.all_to_all(
        x, axis, split_axis=0, concat_axis=0, axis_index_groups=groups, tiled=True
    )


def beside(x, steps):
    pairs = [(i, (i // DEPTH - steps) % SIDES * DEPTH + i % DEPTH) for i in range(OWNERS)]
    return lax.ppermute(x, "adapter", pairs)


def turn(x, chips, cores):
    pairs = [
        (i, (i // CORES + chips) % CHIPS * CORES + (i + cores) % CORES) for i in range(TENSOR)
    ]
    return lax.ppermute(x, "tensor", pairs)


def frozen_sum(attended, out_weight):
    index = lax.axis_index("tensor")
    chip, core = index // CORES, index % CORES
    part = jnp.dot(attended, out_weight, preferred_element_type=F32)
    part = part.reshape(ROWS, CHIPS, CORES, COLS)
    kept = jnp.where(core == 0, part[:, :, 0], part[:, :, 1])
    sent = jnp.where(core == 0, part[:, :, 1], part[:, :, 0]).astype(BF)
    came = turn(sent, 0, 1)
    pair = (kept + came.astype(F32)).reshape(ROWS, CHIPS * COLS)
    rounded = pair.astype(BF)
    total = lax.dynamic_slice_in_dim(pair, chip * COLS, COLS, 1)
    for step in range(1, CHIPS):
        block = lax.dynamic_slice_in_dim(rounded, ((chip + step) % CHIPS) * COLS, COLS, 1)
        total = total + turn(block, step, 0).astype(F32)
    return total


def local(
    queries,
    cache_keys,
    cache_values,
    new_keys,
    new_values,
    cache_lengths,
    out_weight,
    adapter_down,
    adapter_up,
    adapter_ids,
    hub_weights,
):
    attended, payload = attend(
        queries,
        cache_keys.reshape(-1, HEAD_DIM),
        cache_values.reshape(-1, HEAD_DIM),
        new_keys,
        new_values,
        cache_lengths.reshape(1, ROWS),
        adapter_ids.T,
        hub_weights.T,
    )
    got = swap(payload, "adapter")
    frozen = frozen_sum(attended, out_weight)
    picks, record = call(
        pick_kernel,
        (shape_of(PARTS * ROWS, LINES), shape_of(ROWS, 128)),
        adapter_ids.T,
        hub_weights.T,
        attended,
    )
    later_up, attended = lax.optimization_barrier((adapter_up, attended))
    ahead, behind = beside(later_up, 1), beside(later_up, SIDES - 1)
    got, frozen, picks, record = lax.optimization_barrier((got, frozen, picks, record))
    lowered = lower(got, adapter_down)
    lowered = swap(lowered, "adapter")
    far_low, far_high = split(ahead, behind)
    lowered, far_low, far_high = lax.optimization_barrier((lowered, far_low, far_high))
    share = call(home_kernel, shape_of(ROWS // 2, 128, dtype=F32), lowered, picks)
    share = share + turn(share, 0, 1)
    share, far_low, far_high = lax.optimization_barrier((share, far_low, far_high))
    shares = [turn(share, step, 0) for step in (1, CHIPS - 1, 2)]
    ups = (adapter_up, ahead, behind, beside(far_low, 1), beside(far_high, SIDES - 1))
    mixed = call(mix_kernel, shape_of(DEPTH * ROWS, 128), share, *shares, record)
    mixed = swap(mixed, "adapter", COLUMNS)
    place = lax.axis_index("adapter").reshape(1, 1)
    raised = swap(lift(place, mixed, ups), "adapter", COLUMNS)
    return call(final_kernel, shape_of(ROWS, COLS), raised, frozen)


def solution(mesh):
    return jax.shard_map(
        local,
        mesh=mesh,
        in_specs=(
            P("adapter", "tensor"),
            P("adapter", "tensor", None, None),
            P("adapter", "tensor", None, None),
            P("adapter", "tensor"),
            P("adapter", "tensor"),
            P("adapter"),
            P("tensor", None),
            P("tensor", "adapter"),
            P("adapter", "tensor"),
            P("adapter", None),
            P("adapter", None),
        ),
        out_specs=P("adapter", "tensor"),
        check_vma=False,
    )
```

```python
import functools
import math

import jax
import jax.numpy as jnp
from jax import lax
from jax.experimental import pallas as pl
from jax.experimental.pallas import tpu as pltpu
from jax.sharding import PartitionSpec as P

HEADS = 64
KV_HEADS = 8
GROUP = HEADS // KV_HEADS
HEAD_DIM = 128
RANK = 64
ADP_DEV = 16
TOPA = 4
CAP = 24
ROWS = 48
OWNERS = 32
PART = 8
PARTS = CAP // PART
LINES = OWNERS * PART
FEATS = GROUP * HEAD_DIM
COLS = 512
TENSOR = 8
CORES = 2
CHIPS = 4
DOWN_STEPS = 2
PIECES = 2
DEPTH = 8
SIDES = 4
COLUMNS = [[y * DEPTH + z for z in range(DEPTH)] for y in range(SIDES)]
CHUNK = 16
BF = jnp.bfloat16
F32 = jnp.float32


def iota(shape, dim):
    return lax.broadcasted_iota(jnp.int32, shape, dim)


def dot(a, b, contract=((1,), (0,))):
    return lax.dot_general(a, b, (contract, ((), ())), preferred_element_type=F32)


def column(line):
    diagonal = iota((ROWS, ROWS), 0) == iota((ROWS, ROWS), 1)
    return jnp.sum(jnp.where(diagonal, line, 0.0), axis=1, keepdims=True)


def split_parts(x):
    high = x.astype(BF)
    low = (x - high.astype(F32)).astype(BF)
    return high, low


def attend_kernel(
    q_hbm, ck_hbm, cv_hbm, nk_hbm, nv_hbm, lens_hbm, ids_hbm, hub_hbm,
    att, pay,
    picks, q, ck, cv, nk, nv, lens, ids, hub, sems, made, out_sems,
):
    def leave(g, start, width):
        cols = pl.ds(start, width)
        copy = pltpu.make_async_copy(made.at[:, cols], pay.at[:, cols], out_sems.at[g])
        copy.start()
        return copy

    copies = []
    sources = (ids_hbm, hub_hbm, lens_hbm, q_hbm, ck_hbm, nk_hbm, nv_hbm, cv_hbm)
    for n, (src, dst) in enumerate(zip(sources, (ids, hub, lens, q, ck, nk, nv, cv))):
        copies.append(pltpu.make_async_copy(src, dst, sems.at[n]))
        copies[-1].start()

    copies[0].wait()
    copies[1].wait()
    shape = (LINES, ROWS)
    owner_of_line = iota(shape, 0) >> 3
    hits = [(ids[j : j + 1, :] >> 4) == owner_of_line for j in range(TOPA)]
    named = (hits[0] | hits[1]) | (hits[2] | hits[3])
    earlier = (iota((ROWS, ROWS), 0) < iota((ROWS, ROWS), 1)).astype(BF)
    place = dot(named.astype(BF), earlier).astype(jnp.int32)
    place = jnp.where(named, place, -1)
    spot = iota(shape, 0) & (PART - 1)
    line = iota((128, ROWS), 0)
    spreads = []
    for j in range(TOPA):
        within = ids[j : j + 1, :] & (ADP_DEV - 1)
        high, low = split_parts(hub[j : j + 1, :])
        spread = jnp.where(line == within, high.astype(F32), 0.0)
        spread = jnp.where(line == within + ADP_DEV, low.astype(F32), spread)
        spreads.append(spread.astype(BF))
    meta = jnp.zeros((LINES, 128), F32)
    for g in range(PARTS):
        pick = place == spot + g * PART
        picks[pl.ds(g * LINES, LINES), :] = pick.astype(BF)
        coefs = jnp.zeros((LINES, 128), F32)
        for j in range(TOPA):
            coefs = coefs + dot((pick & hits[j]).astype(BF), spreads[j], ((1,), (1,)))
        meta = meta + (pltpu.roll(coefs, g * 2 * ADP_DEV, 1) if g else coefs)
    made[:, PARTS * FEATS :] = meta.astype(BF)
    leaving = [leave(PARTS * PIECES, PARTS * FEATS, 128)]

    for copy in copies[2:]:
        copy.wait()
    lengths = column(lens[...].astype(F32)).astype(jnp.int32)
    scale = 1.0 / math.sqrt(HEAD_DIM)
    keys = CHUNK * 32
    wide = CHUNK * GROUP
    row_of = iota((wide, keys), 0) & (CHUNK - 1)
    col = iota((wide, keys), 1)
    for c in range(ROWS // CHUNK):
        rows = pl.ds(c * CHUNK, CHUNK)
        qc = q[rows, :]
        qs = jnp.concatenate([qc[:, h * HEAD_DIM : (h + 1) * HEAD_DIM] for h in range(GROUP)], axis=0)
        kc = ck[pl.ds(c * keys, keys), :]
        vc = cv[pl.ds(c * keys, keys), :]
        scores = dot(qs, kc, ((1,), (1,))) * scale
        held = jnp.concatenate([lengths[c * CHUNK : (c + 1) * CHUNK, :]] * GROUP, axis=0)
        usable = (row_of == (col >> 5)) & ((col & 31) < held)
        scores = jnp.where(usable, scores, -jnp.inf)
        fresh_k = jnp.concatenate([nk[rows, :].astype(F32)] * GROUP, axis=0)
        fresh_v = jnp.concatenate([nv[rows, :].astype(F32)] * GROUP, axis=0)
        new_scores = jnp.sum(qs.astype(F32) * fresh_k, axis=1, keepdims=True) * scale
        highest = jnp.maximum(jnp.max(scores, axis=1, keepdims=True), new_scores)
        probs = jnp.exp(scores - highest)
        new_probs = jnp.exp(new_scores - highest)
        totals = jnp.sum(probs, axis=1, keepdims=True) + new_probs
        summed = dot(probs.astype(BF), vc) + new_probs.astype(BF).astype(F32) * fresh_v
        out = (summed / totals).astype(BF)
        for h in range(GROUP):
            att[rows, h * HEAD_DIM : (h + 1) * HEAD_DIM] = out[h * CHUNK : (h + 1) * CHUNK, :]
    everything = att[...]
    for g in range(PARTS):
        pick = picks[pl.ds(g * LINES, LINES), :]
        for n in range(PIECES):
            width = FEATS // PIECES
            start = g * FEATS + n * width
            piece = dot(pick, everything[:, n * width : (n + 1) * width])
            made[:, start : start + width] = piece.astype(BF)
            leaving.append(leave(g * PIECES + n, start, width))
    for copy in leaving:
        copy.wait()


def coefs_of(meta, g, first=0, count=ADP_DEV):
    shape = (128, count * RANK)
    line = iota(shape, 0)
    adapter = (iota(shape, 1) >> 6) + first
    spread = (line == adapter + g * 32) | (line == adapter + (g * 32 + ADP_DEV))
    return dot(meta, spread.astype(BF))


def join_parts(pieces):
    lane = iota((pieces[0].shape[0], 128), 1)
    first = jnp.where(lane < RANK, pieces[0], pieces[1])
    second = jnp.where(lane < RANK, pieces[2], 0.0)
    return jnp.concatenate([first, second], axis=1)


def lower_kernel(got, down, out, weights, sems):
    width = down.shape[1] // DOWN_STEPS
    copies = []
    for n in range(DOWN_STEPS):
        cols = pl.ds(n * width, width)
        copies.append(pltpu.make_async_copy(down.at[:, cols], weights.at[:, cols], sems.at[n]))
        copies[-1].start()
    meta = got[:, PARTS * FEATS :]
    coefs = [coefs_of(meta, g) for g in range(PARTS)]
    totals = [jnp.zeros((LINES, 128), F32)] * PARTS
    for n in range(DOWN_STEPS):
        copies[n].wait()
        block = weights[:, n * width : (n + 1) * width]
        for g in range(PARTS):
            lowered = dot(got[:, g * FEATS : (g + 1) * FEATS], block)
            lowered = lowered * coefs[g][:, n * width : (n + 1) * width]
            for p in range(width // 128):
                totals[g] = totals[g] + lowered[:, p * 128 : (p + 1) * 128]
    pieces = [total + pltpu.roll(total, RANK, 1) for total in totals]
    out[...] = join_parts(pieces).astype(BF)


def pick_kernel(ids, hub, after, picks, record):
    owner_of_line = iota((ROWS, LINES), 1) >> 3
    named = jnp.zeros((ROWS, LINES), jnp.bool_)
    lane = iota((ROWS, 128), 1) - RANK
    kept = jnp.zeros((ROWS, 128), F32)
    for j in range(TOPA):
        adapter = column(ids[j : j + 1, :].astype(F32)).astype(jnp.int32)
        owner = adapter >> 4
        named = named | (owner == owner_of_line)
        high, low = split_parts(column(hub[j : j + 1, :]))
        fields = (owner.astype(F32), (adapter & (ADP_DEV - 1)).astype(F32), high.astype(F32), low.astype(F32))
        for k, field in enumerate(fields):
            kept = jnp.where(lane == k * TOPA + j, field, kept)
    record[...] = kept.astype(BF)
    earlier = (iota((ROWS, ROWS), 1) < iota((ROWS, ROWS), 0)).astype(BF)
    place = dot(earlier, named.astype(BF)).astype(jnp.int32)
    place = jnp.where(named, place, -1)
    spot = iota((ROWS, LINES), 1) & (PART - 1)
    for g in range(PARTS):
        picks[pl.ds(g * ROWS, ROWS), :] = (place == spot + g * PART).astype(BF)


def split_kernel(ahead, behind, far_low, far_high, sems):
    half = far_low.shape[0]
    copies = [
        pltpu.make_async_copy(ahead.at[pl.ds(0, half), :], far_low, sems.at[0]),
        pltpu.make_async_copy(behind.at[pl.ds(half, half), :], far_high, sems.at[1]),
    ]
    for copy in copies:
        copy.start()
    for copy in copies:
        copy.wait()


def home_kernel(got, picks, out):
    lane = iota((ROWS, 256), 1)
    total = jnp.zeros((ROWS, 256), F32)
    for g in range(PARTS):
        part = dot(picks[pl.ds(g * ROWS, ROWS), :], got[...])
        total = total + jnp.where((lane >> 6) == g, part, 0.0)
    folded = total[:, :128] + total[:, 128:]
    folded = folded + pltpu.roll(folded, RANK, 1)
    half = ROWS // 2
    lane = iota((half, 128), 1)
    out[...] = jnp.where(lane < RANK, folded[:half, :], folded[half:, :])


def mix_kernel(own, ahead, behind, across, record, out):
    half = ROWS // 2
    total = (own[...] + ahead[...]) + (behind[...] + across[...])
    other = pltpu.roll(total, RANK, 1)
    mixed = jnp.concatenate([total, other], axis=0)
    lane = iota((ROWS, 128), 1)
    sent = jnp.where(lane < RANK, mixed, record[...].astype(F32)).astype(BF)
    for z in range(DEPTH):
        out[pl.ds(z * ROWS, ROWS), :] = sent


def raise_kernel(place, got, *refs):
    ups, (out, held, sems) = refs[: SIDES + 1], refs[SIDES + 1 :]
    half = held.shape[1] // 2
    copies = []
    for b in range(SIDES + 1):
        if b < SIDES - 1:
            target = held.at[b]
        else:
            target = held.at[SIDES - 1, pl.ds((b - SIDES + 1) * half, half), :]
        copies.append(pltpu.make_async_copy(ups[b], target, sems.at[b]))
        copies[-1].start()
    me = place[0, 0]
    y, z = me >> 3, me & (DEPTH - 1)
    rows = DEPTH * ROWS
    lane = iota((1, 128), 1)
    spot = lane & (RANK - 1)
    side = spot >> 4
    away = jnp.where(side == 3, 2, jnp.where(side == 2, 3, side))
    wanted = ((((y + away) & (SIDES - 1)) * DEPTH + z) * ADP_DEV + (spot & (ADP_DEV - 1))).astype(F32)
    record = got[...].astype(F32)
    lanes = iota((rows, 128), 1)
    coef = jnp.zeros((rows, 128), F32)
    for j in range(TOPA):
        owner, local, high, low = (
            record[:, RANK + k * TOPA + j : RANK + k * TOPA + j + 1] for k in range(4)
        )
        weight = jnp.where(lanes < RANK, high, low)
        coef = jnp.where(owner * ADP_DEV + local == wanted, weight, coef)
    coef = coef.astype(BF)
    mixed = jnp.where(lanes < RANK, record, pltpu.roll(record, RANK, 1))
    shape = (128, ADP_DEV * RANK)
    line = iota(shape, 0) & (RANK - 1)
    adapter = iota(shape, 1) >> 6
    blocks = []
    for b in range(SIDES):
        coefs = dot(coef, (line == adapter + b * ADP_DEV).astype(BF))
        for p in range(ADP_DEV * RANK // 128):
            blocks.append((coefs[:, p * 128 : (p + 1) * 128] * mixed).astype(BF))
    for copy in copies:
        copy.wait()
    total = dot(jnp.concatenate(blocks, axis=1), held[...].reshape(SIDES * ADP_DEV * RANK, COLS))
    out[...] = total.astype(BF)


def final_kernel(got, frozen, out):
    total = frozen[...]
    for z in range(DEPTH):
        total = total + got[pl.ds(z * ROWS, ROWS), :].astype(F32)
    out[...] = total.astype(BF)


def split(ahead, behind):
    half = shape_of(ahead.shape[0] // 2, ahead.shape[1])
    hbm = pl.BlockSpec(memory_space=pltpu.HBM)
    return pl.pallas_call(
        split_kernel,
        out_shape=(half, half),
        in_specs=[hbm, hbm],
        out_specs=(hbm, hbm),
        scratch_shapes=[pltpu.SemaphoreType.DMA((2,))],
        compiler_params=pltpu.CompilerParams(vmem_limit_bytes=24 * 1024 * 1024),
    )(*[pltpu.with_memory_space_constraint(x, pltpu.HBM) for x in (ahead, behind)])


def lift(place, got, ups):
    return pl.pallas_call(
        raise_kernel,
        out_shape=shape_of(DEPTH * ROWS, COLS),
        in_specs=[pl.BlockSpec(memory_space=pltpu.SMEM), pl.BlockSpec(memory_space=pltpu.VMEM)]
        + [pl.BlockSpec(memory_space=pltpu.HBM)] * 3
        + [pl.BlockSpec(memory_space=pl.ANY)] * 2,
        scratch_shapes=[
            pltpu.VMEM((SIDES, *ups[0].shape), BF),
            pltpu.SemaphoreType.DMA((len(ups),)),
        ],
        compiler_params=pltpu.CompilerParams(vmem_limit_bytes=32 * 1024 * 1024),
    )(place, got, *[pltpu.with_memory_space_constraint(up, pltpu.HBM) for up in ups[:3]], *ups[3:])


def attend(*args):
    return pl.pallas_call(
        attend_kernel,
        out_shape=(
            shape_of(ROWS, FEATS),
            shape_of(LINES, PARTS * FEATS + 128),
        ),
        in_specs=[pl.BlockSpec(memory_space=pltpu.HBM)] * len(args),
        out_specs=(
            pl.BlockSpec(memory_space=pltpu.VMEM),
            pl.BlockSpec(memory_space=pltpu.HBM),
        ),
        scratch_shapes=[pltpu.VMEM((PARTS * LINES, ROWS), BF)]
        + [pltpu.VMEM(x.shape, x.dtype) for x in args]
        + [
            pltpu.SemaphoreType.DMA((len(args),)),
            pltpu.VMEM((LINES, PARTS * FEATS + 128), BF),
            pltpu.SemaphoreType.DMA((PARTS * PIECES + 1,)),
        ],
        compiler_params=pltpu.CompilerParams(vmem_limit_bytes=32 * 1024 * 1024),
    )(*[pltpu.with_memory_space_constraint(x, pltpu.HBM) for x in args])


def lower(got, down):
    return pl.pallas_call(
        lower_kernel,
        out_shape=shape_of(LINES, 256),
        in_specs=[pl.BlockSpec(memory_space=pltpu.VMEM), pl.BlockSpec(memory_space=pltpu.HBM)],
        scratch_shapes=[
            pltpu.VMEM(down.shape, down.dtype),
            pltpu.SemaphoreType.DMA((DOWN_STEPS,)),
        ],
        compiler_params=pltpu.CompilerParams(vmem_limit_bytes=24 * 1024 * 1024),
    )(got, pltpu.with_memory_space_constraint(down, pltpu.HBM))


def call(kernel, out_shape, *args):
    return pl.pallas_call(
        kernel,
        out_shape=out_shape,
        compiler_params=pltpu.CompilerParams(vmem_limit_bytes=24 * 1024 * 1024),
    )(*args)


def shape_of(*shape, dtype=BF):
    return jax.ShapeDtypeStruct(shape, dtype)


def swap(x, axis, groups=None):
    return lax.all_to_all(
        x, axis, split_axis=0, concat_axis=0, axis_index_groups=groups, tiled=True
    )


def beside(x, steps):
    pairs = [(i, (i // DEPTH - steps) % SIDES * DEPTH + i % DEPTH) for i in range(OWNERS)]
    return lax.ppermute(x, "adapter", pairs)


def turn(x, chips, cores):
    pairs = [
        (i, (i // CORES + chips) % CHIPS * CORES + (i + cores) % CORES) for i in range(TENSOR)
    ]
    return lax.ppermute(x, "tensor", pairs)


def frozen_sum(attended, out_weight):
    index = lax.axis_index("tensor")
    chip, core = index // CORES, index % CORES
    part = jnp.dot(attended, out_weight, preferred_element_type=F32)
    part = part.reshape(ROWS, CHIPS, CORES, COLS)
    kept = jnp.where(core == 0, part[:, :, 0], part[:, :, 1])
    sent = jnp.where(core == 0, part[:, :, 1], part[:, :, 0]).astype(BF)
    came = turn(sent, 0, 1)
    pair = (kept + came.astype(F32)).reshape(ROWS, CHIPS * COLS)
    rounded = pair.astype(BF)
    total = lax.dynamic_slice_in_dim(pair, chip * COLS, COLS, 1)
    for step in range(1, CHIPS):
        block = lax.dynamic_slice_in_dim(rounded, ((chip + step) % CHIPS) * COLS, COLS, 1)
        total = total + turn(block, step, 0).astype(F32)
    return total


def local(
    queries,
    cache_keys,
    cache_values,
    new_keys,
    new_values,
    cache_lengths,
    out_weight,
    adapter_down,
    adapter_up,
    adapter_ids,
    hub_weights,
):
    attended, payload = attend(
        queries,
        cache_keys.reshape(-1, HEAD_DIM),
        cache_values.reshape(-1, HEAD_DIM),
        new_keys,
        new_values,
        cache_lengths.reshape(1, ROWS),
        adapter_ids.T,
        hub_weights.T,
    )
    got = swap(payload, "adapter")
    frozen = frozen_sum(attended, out_weight)
    picks, record = call(
        pick_kernel,
        (shape_of(PARTS * ROWS, LINES), shape_of(ROWS, 128)),
        adapter_ids.T,
        hub_weights.T,
        attended,
    )
    later_up, attended = lax.optimization_barrier((adapter_up, attended))
    ahead, behind = beside(later_up, 1), beside(later_up, SIDES - 1)
    got, frozen, picks, record = lax.optimization_barrier((got, frozen, picks, record))
    lowered = lower(got, adapter_down)
    lowered = swap(lowered, "adapter")
    far_low, far_high = split(ahead, behind)
    lowered, far_low, far_high = lax.optimization_barrier((lowered, far_low, far_high))
    share = call(home_kernel, shape_of(ROWS // 2, 128, dtype=F32), lowered, picks)
    share = share + turn(share, 0, 1)
    share, far_low, far_high = lax.optimization_barrier((share, far_low, far_high))
    shares = [turn(share, step, 0) for step in (1, CHIPS - 1, 2)]
    ups = (adapter_up, ahead, behind, beside(far_low, 1), beside(far_high, SIDES - 1))
    mixed = call(mix_kernel, shape_of(DEPTH * ROWS, 128), share, *shares, record)
    mixed = swap(mixed, "adapter", COLUMNS)
    place = lax.axis_index("adapter").reshape(1, 1)
    raised = swap(lift(place, mixed, ups), "adapter", COLUMNS)
    return call(final_kernel, shape_of(ROWS, COLS), raised, frozen)


def solution(mesh):
    return jax.shard_map(
        local,
        mesh=mesh,
        in_specs=(
            P("adapter", "tensor"),
            P("adapter", "tensor", None, None),
            P("adapter", "tensor", None, None),
            P("adapter", "tensor"),
            P("adapter", "tensor"),
            P("adapter"),
            P("tensor", None),
            P("tensor", "adapter"),
            P("adapter", "tensor"),
            P("adapter", None),
            P("adapter", None),
        ),
        out_specs=P("adapter", "tensor"),
        check_vma=False,
    )
```

```python
import functools
import math

import jax
import jax.numpy as jnp
from jax import lax
from jax.experimental import pallas as pl
from jax.experimental.pallas import tpu as pltpu
from jax.sharding import PartitionSpec as P

HEADS = 64
KV_HEADS = 8
GROUP = HEADS // KV_HEADS
HEAD_DIM = 128
RANK = 64
ADP_DEV = 16
TOPA = 4
CAP = 24
ROWS = 48
OWNERS = 32
PART = 8
PARTS = CAP // PART
LINES = OWNERS * PART
FEATS = GROUP * HEAD_DIM
COLS = 512
TENSOR = 8
CORES = 2
CHIPS = 4
DOWN_STEPS = 2
PIECES = 2
DEPTH = 8
SIDES = 4
COLUMNS = [[y * DEPTH + z for z in range(DEPTH)] for y in range(SIDES)]
CHUNK = 16
BF = jnp.bfloat16
F32 = jnp.float32


def iota(shape, dim):
    return lax.broadcasted_iota(jnp.int32, shape, dim)


def dot(a, b, contract=((1,), (0,))):
    return lax.dot_general(a, b, (contract, ((), ())), preferred_element_type=F32)


def column(line):
    diagonal = iota((ROWS, ROWS), 0) == iota((ROWS, ROWS), 1)
    return jnp.sum(jnp.where(diagonal, line, 0.0), axis=1, keepdims=True)


def split_parts(x):
    high = x.astype(BF)
    low = (x - high.astype(F32)).astype(BF)
    return high, low


def attend_kernel(
    q_hbm, ck_hbm, cv_hbm, nk_hbm, nv_hbm, lens_hbm, ids_hbm, hub_hbm,
    att, pay,
    picks, q, ck, cv, nk, nv, lens, ids, hub, sems, made, out_sems,
):
    def leave(g, start, width):
        cols = pl.ds(start, width)
        copy = pltpu.make_async_copy(made.at[:, cols], pay.at[:, cols], out_sems.at[g])
        copy.start()
        return copy

    copies = []
    sources = (ids_hbm, hub_hbm, lens_hbm, q_hbm, ck_hbm, nk_hbm, nv_hbm, cv_hbm)
    for n, (src, dst) in enumerate(zip(sources, (ids, hub, lens, q, ck, nk, nv, cv))):
        copies.append(pltpu.make_async_copy(src, dst, sems.at[n]))
        copies[-1].start()

    copies[0].wait()
    copies[1].wait()
    shape = (LINES, ROWS)
    owner_of_line = iota(shape, 0) >> 3
    hits = [(ids[j : j + 1, :] >> 4) == owner_of_line for j in range(TOPA)]
    named = (hits[0] | hits[1]) | (hits[2] | hits[3])
    earlier = (iota((ROWS, ROWS), 0) < iota((ROWS, ROWS), 1)).astype(BF)
    place = dot(named.astype(BF), earlier).astype(jnp.int32)
    place = jnp.where(named, place, -1)
    spot = iota(shape, 0) & (PART - 1)
    line = iota((128, ROWS), 0)
    spreads = []
    for j in range(TOPA):
        within = ids[j : j + 1, :] & (ADP_DEV - 1)
        high, low = split_parts(hub[j : j + 1, :])
        spread = jnp.where(line == within, high.astype(F32), 0.0)
        spread = jnp.where(line == within + ADP_DEV, low.astype(F32), spread)
        spreads.append(spread.astype(BF))
    meta = jnp.zeros((LINES, 128), F32)
    for g in range(PARTS):
        pick = place == spot + g * PART
        picks[pl.ds(g * LINES, LINES), :] = pick.astype(BF)
        coefs = jnp.zeros((LINES, 128), F32)
        for j in range(TOPA):
            coefs = coefs + dot((pick & hits[j]).astype(BF), spreads[j], ((1,), (1,)))
        meta = meta + (pltpu.roll(coefs, g * 2 * ADP_DEV, 1) if g else coefs)
    made[:, PARTS * FEATS :] = meta.astype(BF)
    leaving = [leave(PARTS * PIECES, PARTS * FEATS, 128)]

    for copy in copies[2:]:
        copy.wait()
    lengths = column(lens[...].astype(F32)).astype(jnp.int32)
    scale = 1.0 / math.sqrt(HEAD_DIM)
    keys = CHUNK * 32
    wide = CHUNK * GROUP
    row_of = iota((wide, keys), 0) & (CHUNK - 1)
    col = iota((wide, keys), 1)
    for c in range(ROWS // CHUNK):
        rows = pl.ds(c * CHUNK, CHUNK)
        qc = q[rows, :]
        qs = jnp.concatenate([qc[:, h * HEAD_DIM : (h + 1) * HEAD_DIM] for h in range(GROUP)], axis=0)
        kc = ck[pl.ds(c * keys, keys), :]
        vc = cv[pl.ds(c * keys, keys), :]
        scores = dot(qs, kc, ((1,), (1,))) * scale
        held = jnp.concatenate([lengths[c * CHUNK : (c + 1) * CHUNK, :]] * GROUP, axis=0)
        usable = (row_of == (col >> 5)) & ((col & 31) < held)
        scores = jnp.where(usable, scores, -jnp.inf)
        fresh_k = jnp.concatenate([nk[rows, :].astype(F32)] * GROUP, axis=0)
        fresh_v = jnp.concatenate([nv[rows, :].astype(F32)] * GROUP, axis=0)
        new_scores = jnp.sum(qs.astype(F32) * fresh_k, axis=1, keepdims=True) * scale
        highest = jnp.maximum(jnp.max(scores, axis=1, keepdims=True), new_scores)
        probs = jnp.exp(scores - highest)
        new_probs = jnp.exp(new_scores - highest)
        totals = jnp.sum(probs, axis=1, keepdims=True) + new_probs
        summed = dot(probs.astype(BF), vc) + new_probs.astype(BF).astype(F32) * fresh_v
        out = (summed / totals).astype(BF)
        for h in range(GROUP):
            att[rows, h * HEAD_DIM : (h + 1) * HEAD_DIM] = out[h * CHUNK : (h + 1) * CHUNK, :]
    everything = att[...]
    for g in range(PARTS):
        pick = picks[pl.ds(g * LINES, LINES), :]
        for n in range(PIECES):
            width = FEATS // PIECES
            start = g * FEATS + n * width
            piece = dot(pick, everything[:, n * width : (n + 1) * width])
            made[:, start : start + width] = piece.astype(BF)
            leaving.append(leave(g * PIECES + n, start, width))
    for copy in leaving:
        copy.wait()


def coefs_of(meta, g, first=0, count=ADP_DEV):
    shape = (128, count * RANK)
    line = iota(shape, 0)
    adapter = (iota(shape, 1) >> 6) + first
    spread = (line == adapter + g * 32) | (line == adapter + (g * 32 + ADP_DEV))
    return dot(meta, spread.astype(BF))


def join_parts(pieces):
    lane = iota((pieces[0].shape[0], 128), 1)
    first = jnp.where(lane < RANK, pieces[0], pieces[1])
    second = jnp.where(lane < RANK, pieces[2], 0.0)
    return jnp.concatenate([first, second], axis=1)


def lower_kernel(got, down, out, weights, sems):
    width = down.shape[1] // DOWN_STEPS
    copies = []
    for n in range(DOWN_STEPS):
        cols = pl.ds(n * width, width)
        copies.append(pltpu.make_async_copy(down.at[:, cols], weights.at[:, cols], sems.at[n]))
        copies[-1].start()
    meta = got[:, PARTS * FEATS :]
    coefs = [coefs_of(meta, g) for g in range(PARTS)]
    totals = [jnp.zeros((LINES, 128), F32)] * PARTS
    for n in range(DOWN_STEPS):
        copies[n].wait()
        block = weights[:, n * width : (n + 1) * width]
        for g in range(PARTS):
            lowered = dot(got[:, g * FEATS : (g + 1) * FEATS], block)
            lowered = lowered * coefs[g][:, n * width : (n + 1) * width]
            for p in range(width // 128):
                totals[g] = totals[g] + lowered[:, p * 128 : (p + 1) * 128]
    pieces = [total + pltpu.roll(total, RANK, 1) for total in totals]
    out[...] = join_parts(pieces).astype(BF)


def pick_kernel(ids, hub, after, picks, record):
    owner_of_line = iota((ROWS, LINES), 1) >> 3
    named = jnp.zeros((ROWS, LINES), jnp.bool_)
    lane = iota((ROWS, 128), 1) - RANK
    kept = jnp.zeros((ROWS, 128), F32)
    for j in range(TOPA):
        adapter = column(ids[j : j + 1, :].astype(F32)).astype(jnp.int32)
        owner = adapter >> 4
        named = named | (owner == owner_of_line)
        high, low = split_parts(column(hub[j : j + 1, :]))
        fields = (owner.astype(F32), (adapter & (ADP_DEV - 1)).astype(F32), high.astype(F32), low.astype(F32))
        for k, field in enumerate(fields):
            kept = jnp.where(lane == k * TOPA + j, field, kept)
    record[...] = kept.astype(BF)
    earlier = (iota((ROWS, ROWS), 1) < iota((ROWS, ROWS), 0)).astype(BF)
    place = dot(earlier, named.astype(BF)).astype(jnp.int32)
    place = jnp.where(named, place, -1)
    spot = iota((ROWS, LINES), 1) & (PART - 1)
    for g in range(PARTS):
        picks[pl.ds(g * ROWS, ROWS), :] = (place == spot + g * PART).astype(BF)


def split_kernel(ahead, behind, far_low, far_high, sems):
    half = far_low.shape[0]
    copies = [
        pltpu.make_async_copy(ahead.at[pl.ds(0, half), :], far_low, sems.at[0]),
        pltpu.make_async_copy(behind.at[pl.ds(half, half), :], far_high, sems.at[1]),
    ]
    for copy in copies:
        copy.start()
    for copy in copies:
        copy.wait()


def home_kernel(got, picks, out):
    lane = iota((ROWS, 256), 1)
    total = jnp.zeros((ROWS, 256), F32)
    for g in range(PARTS):
        part = dot(picks[pl.ds(g * ROWS, ROWS), :], got[...])
        total = total + jnp.where((lane >> 6) == g, part, 0.0)
    folded = total[:, :128] + total[:, 128:]
    folded = folded + pltpu.roll(folded, RANK, 1)
    half = ROWS // 2
    lane = iota((half, 128), 1)
    out[...] = jnp.where(lane < RANK, folded[:half, :], folded[half:, :])


def mix_kernel(own, ahead, behind, across, record, out):
    half = ROWS // 2
    total = (own[...] + ahead[...]) + (behind[...] + across[...])
    other = pltpu.roll(total, RANK, 1)
    mixed = jnp.concatenate([total, other], axis=0)
    lane = iota((ROWS, 128), 1)
    sent = jnp.where(lane < RANK, mixed, record[...].astype(F32)).astype(BF)
    for z in range(DEPTH):
        out[pl.ds(z * ROWS, ROWS), :] = sent


def raise_kernel(place, got, *refs):
    ups, (out, held, sems) = refs[: SIDES + 1], refs[SIDES + 1 :]
    half = held.shape[1] // 2
    copies = []
    for b in range(SIDES + 1):
        if b < SIDES - 1:
            target = held.at[b]
        else:
            target = held.at[SIDES - 1, pl.ds((b - SIDES + 1) * half, half), :]
        copies.append(pltpu.make_async_copy(ups[b], target, sems.at[b]))
        copies[-1].start()
    me = place[0, 0]
    y, z = me >> 3, me & (DEPTH - 1)
    rows = DEPTH * ROWS
    lane = iota((1, 128), 1)
    spot = lane & (RANK - 1)
    side = spot >> 4
    away = jnp.where(side == 3, 2, jnp.where(side == 2, 3, side))
    wanted = ((((y + away) & (SIDES - 1)) * DEPTH + z) * ADP_DEV + (spot & (ADP_DEV - 1))).astype(F32)
    record = got[...].astype(F32)
    lanes = iota((rows, 128), 1)
    coef = jnp.zeros((rows, 128), F32)
    for j in range(TOPA):
        owner, local, high, low = (
            record[:, RANK + k * TOPA + j : RANK + k * TOPA + j + 1] for k in range(4)
        )
        weight = jnp.where(lanes < RANK, high, low)
        coef = jnp.where(owner * ADP_DEV + local == wanted, weight, coef)
    coef = coef.astype(BF)
    mixed = jnp.where(lanes < RANK, record, pltpu.roll(record, RANK, 1))
    shape = (128, ADP_DEV * RANK)
    line = iota(shape, 0) & (RANK - 1)
    adapter = iota(shape, 1) >> 6
    blocks = []
    for b in range(SIDES):
        coefs = dot(coef, (line == adapter + b * ADP_DEV).astype(BF))
        for p in range(ADP_DEV * RANK // 128):
            blocks.append((coefs[:, p * 128 : (p + 1) * 128] * mixed).astype(BF))
    depth = SIDES * ADP_DEV * RANK // 2
    middle = len(blocks) // 2
    for copy in copies[: SIDES // 2]:
        copy.wait()
    near = held[pl.ds(0, SIDES // 2), :, :].reshape(depth, COLS)
    total = dot(jnp.concatenate(blocks[:middle], axis=1), near)
    for copy in copies[SIDES // 2 :]:
        copy.wait()
    rest = held[pl.ds(SIDES // 2, SIDES // 2), :, :].reshape(depth, COLS)
    total = total + dot(jnp.concatenate(blocks[middle:], axis=1), rest)
    out[...] = total.astype(BF)


def final_kernel(got, frozen, out):
    total = frozen[...]
    for z in range(DEPTH):
        total = total + got[pl.ds(z * ROWS, ROWS), :].astype(F32)
    out[...] = total.astype(BF)


def split(ahead, behind):
    half = shape_of(ahead.shape[0] // 2, ahead.shape[1])
    hbm = pl.BlockSpec(memory_space=pltpu.HBM)
    return pl.pallas_call(
        split_kernel,
        out_shape=(half, half),
        in_specs=[hbm, hbm],
        out_specs=(hbm, hbm),
        scratch_shapes=[pltpu.SemaphoreType.DMA((2,))],
        compiler_params=pltpu.CompilerParams(vmem_limit_bytes=24 * 1024 * 1024),
    )(*[pltpu.with_memory_space_constraint(x, pltpu.HBM) for x in (ahead, behind)])


def lift(place, got, ups):
    return pl.pallas_call(
        raise_kernel,
        out_shape=shape_of(DEPTH * ROWS, COLS),
        in_specs=[pl.BlockSpec(memory_space=pltpu.SMEM), pl.BlockSpec(memory_space=pltpu.VMEM)]
        + [pl.BlockSpec(memory_space=pltpu.HBM)] * 3
        + [pl.BlockSpec(memory_space=pl.ANY)] * 2,
        scratch_shapes=[
            pltpu.VMEM((SIDES, *ups[0].shape), BF),
            pltpu.SemaphoreType.DMA((len(ups),)),
        ],
        compiler_params=pltpu.CompilerParams(vmem_limit_bytes=32 * 1024 * 1024),
    )(place, got, *[pltpu.with_memory_space_constraint(up, pltpu.HBM) for up in ups[:3]], *ups[3:])


def attend(*args):
    return pl.pallas_call(
        attend_kernel,
        out_shape=(
            shape_of(ROWS, FEATS),
            shape_of(LINES, PARTS * FEATS + 128),
        ),
        in_specs=[pl.BlockSpec(memory_space=pltpu.HBM)] * len(args),
        out_specs=(
            pl.BlockSpec(memory_space=pltpu.VMEM),
            pl.BlockSpec(memory_space=pltpu.HBM),
        ),
        scratch_shapes=[pltpu.VMEM((PARTS * LINES, ROWS), BF)]
        + [pltpu.VMEM(x.shape, x.dtype) for x in args]
        + [
            pltpu.SemaphoreType.DMA((len(args),)),
            pltpu.VMEM((LINES, PARTS * FEATS + 128), BF),
            pltpu.SemaphoreType.DMA((PARTS * PIECES + 1,)),
        ],
        compiler_params=pltpu.CompilerParams(vmem_limit_bytes=32 * 1024 * 1024),
    )(*[pltpu.with_memory_space_constraint(x, pltpu.HBM) for x in args])


def lower(got, down):
    return pl.pallas_call(
        lower_kernel,
        out_shape=shape_of(LINES, 256),
        in_specs=[pl.BlockSpec(memory_space=pltpu.VMEM), pl.BlockSpec(memory_space=pltpu.HBM)],
        scratch_shapes=[
            pltpu.VMEM(down.shape, down.dtype),
            pltpu.SemaphoreType.DMA((DOWN_STEPS,)),
        ],
        compiler_params=pltpu.CompilerParams(vmem_limit_bytes=24 * 1024 * 1024),
    )(got, pltpu.with_memory_space_constraint(down, pltpu.HBM))


def call(kernel, out_shape, *args):
    return pl.pallas_call(
        kernel,
        out_shape=out_shape,
        compiler_params=pltpu.CompilerParams(vmem_limit_bytes=24 * 1024 * 1024),
    )(*args)


def shape_of(*shape, dtype=BF):
    return jax.ShapeDtypeStruct(shape, dtype)


def swap(x, axis, groups=None):
    return lax.all_to_all(
        x, axis, split_axis=0, concat_axis=0, axis_index_groups=groups, tiled=True
    )


def beside(x, steps):
    pairs = [(i, (i // DEPTH - steps) % SIDES * DEPTH + i % DEPTH) for i in range(OWNERS)]
    return lax.ppermute(x, "adapter", pairs)


def turn(x, chips, cores):
    pairs = [
        (i, (i // CORES + chips) % CHIPS * CORES + (i + cores) % CORES) for i in range(TENSOR)
    ]
    return lax.ppermute(x, "tensor", pairs)


def frozen_sum(attended, out_weight):
    index = lax.axis_index("tensor")
    chip, core = index // CORES, index % CORES
    part = jnp.dot(attended, out_weight, preferred_element_type=F32)
    part = part.reshape(ROWS, CHIPS, CORES, COLS)
    kept = jnp.where(core == 0, part[:, :, 0], part[:, :, 1])
    sent = jnp.where(core == 0, part[:, :, 1], part[:, :, 0]).astype(BF)
    came = turn(sent, 0, 1)
    pair = (kept + came.astype(F32)).reshape(ROWS, CHIPS * COLS)
    rounded = pair.astype(BF)
    total = lax.dynamic_slice_in_dim(pair, chip * COLS, COLS, 1)
    for step in range(1, CHIPS):
        block = lax.dynamic_slice_in_dim(rounded, ((chip + step) % CHIPS) * COLS, COLS, 1)
        total = total + turn(block, step, 0).astype(F32)
    return total


def local(
    queries,
    cache_keys,
    cache_values,
    new_keys,
    new_values,
    cache_lengths,
    out_weight,
    adapter_down,
    adapter_up,
    adapter_ids,
    hub_weights,
):
    attended, payload = attend(
        queries,
        cache_keys.reshape(-1, HEAD_DIM),
        cache_values.reshape(-1, HEAD_DIM),
        new_keys,
        new_values,
        cache_lengths.reshape(1, ROWS),
        adapter_ids.T,
        hub_weights.T,
    )
    got = swap(payload, "adapter")
    frozen = frozen_sum(attended, out_weight)
    picks, record = call(
        pick_kernel,
        (shape_of(PARTS * ROWS, LINES), shape_of(ROWS, 128)),
        adapter_ids.T,
        hub_weights.T,
        attended,
    )
    later_up, attended = lax.optimization_barrier((adapter_up, attended))
    ahead, behind = beside(later_up, 1), beside(later_up, SIDES - 1)
    got, frozen, picks, record = lax.optimization_barrier((got, frozen, picks, record))
    lowered = lower(got, adapter_down)
    lowered = swap(lowered, "adapter")
    far_low, far_high = split(ahead, behind)
    lowered, far_low, far_high = lax.optimization_barrier((lowered, far_low, far_high))
    share = call(home_kernel, shape_of(ROWS // 2, 128, dtype=F32), lowered, picks)
    share = share + turn(share, 0, 1)
    share, far_low, far_high = lax.optimization_barrier((share, far_low, far_high))
    shares = [turn(share, step, 0) for step in (1, CHIPS - 1, 2)]
    ups = (adapter_up, ahead, behind, beside(far_low, 1), beside(far_high, SIDES - 1))
    mixed = call(mix_kernel, shape_of(DEPTH * ROWS, 128), share, *shares, record)
    mixed = swap(mixed, "adapter", COLUMNS)
    place = lax.axis_index("adapter").reshape(1, 1)
    raised = swap(lift(place, mixed, ups), "adapter", COLUMNS)
    return call(final_kernel, shape_of(ROWS, COLS), raised, frozen)


def solution(mesh):
    return jax.shard_map(
        local,
        mesh=mesh,
        in_specs=(
            P("adapter", "tensor"),
            P("adapter", "tensor", None, None),
            P("adapter", "tensor", None, None),
            P("adapter", "tensor"),
            P("adapter", "tensor"),
            P("adapter"),
            P("tensor", None),
            P("tensor", "adapter"),
            P("adapter", "tensor"),
            P("adapter", None),
            P("adapter", None),
        ),
        out_specs=P("adapter", "tensor"),
        check_vma=False,
    )
```
